256 devices in a mesh: row: 32 (over x_lo, z, core), col: 8 (over x_hi, y).
Axes of the slice: x: 4 (x_hi: 2, x_lo: 2; x = x_hi * 2 + x_lo), y: 4, z: 8, core: 2. Of those that a mesh axis runs over, the one named last changes fastest.
Arguments:
- points: bfloat16 [98304, 64], P(('row', 'col')), may hold values from -6 to 6
- panel: bfloat16 [98304, 16], P(('row', 'col')), may hold values from -6 to 6
- tile_pairs: int32 [768, 768], P('row'), may hold values from 0 to 1, as said below
Outputs:
- applied: float32 [98304, 16], P(('row', 'col'))
The draws below stay inside these ranges and needn't reach their ends.
Inputs may be any that keep to these rules, and one draw needn't show every extreme that they name: Each tile belongs to one of 6 clusters arranged in a cycle; tile_pairs[a, b] == 1 exactly when the clusters of tiles a and b are the same or neighbours in that cycle, so it is symmetric with ones on the diagonal.
All inputs are finite; a program needn't handle non-finite values.
Results may differ from the reference program's by a relative error of at most 0.0029.
Values may be sent and summed in bfloat16 or wider, within the bound.
A program may use at most 64 MiB of HBM per device.

```python
import jax
import jax.numpy as jnp
from jax import lax

D = 64
P_SIZE = 16
TILE = 128
NPTS = 98304
TILES = 768


def draw_tile_pairs(key, part):
    key = jax.random.fold_in(key, 5)
    labels = jax.random.randint(key, (TILES,), 0, 6, dtype=jnp.int32)
    apart = (labels[:, None] - labels[None, :]) % 6
    near = (apart == 0) | (apart == 1) | (apart == 5)
    return jnp.where(near, 1, 0).astype(jnp.int32)


def levels(stream_key, extent, split, least, high):
    def one(dim, parts):
        draws = jax.random.uniform(jax.random.fold_in(jax.random.fold_in(stream_key, 6), dim), (parts,), jnp.float32, least / len(split), high / len(split))
        return jnp.repeat(jnp.exp(draws), extent[dim] // parts).reshape((-1,) + (1,) * (len(extent) - dim - 1))

    loudness = one(*split[0])
    for cut in split[1:]:
        loudness = loudness * one(*cut)
    return loudness


def normal_values(stream_key, shape, width, limit, shards=(), kind=jnp.bfloat16):
    gain = levels(stream_key, shape, shards, -0.22, 0.18) if shards else 1.0
    values = jax.random.normal(stream_key, shape, jnp.float32) * width * gain
    return jnp.minimum(jnp.maximum(values, -limit), limit).astype(kind)


def setup_inputs(seed: int = 0) -> dict:
    key_of = jax.random.split(jax.random.key(seed), 4)
    return {
        "points": normal_values(key_of[0], (NPTS, D), 1.0, 6.0, ((0, 256),)),
        "panel": normal_values(key_of[1], (NPTS, P_SIZE), 1.0, 6.0, ((0, 256),)),
        "tile_pairs": draw_tile_pairs(jax.random.fold_in(key_of[3], 71), 0),
    }


def reference(points, panel, tile_pairs):
    total = points.shape[0]
    tiles = total // TILE
    floats = points.astype(jnp.float32)
    norms = jnp.sum(floats * floats, axis=1)
    block_rows = min(512, total)
    block_tiles = block_rows // TILE

    def one_block(index):
        start = index * block_rows
        rows = lax.dynamic_slice_in_dim(points, start, block_rows, 0)
        row_norms = lax.dynamic_slice_in_dim(norms, start, block_rows, 0)
        cross = lax.dot_general(rows, points, (((1,), (1,)), ((), ())), preferred_element_type=jnp.float32)
        dist = jnp.maximum(row_norms[:, None] + norms[None, :] - 2.0 * cross, 0.0)
        values = jnp.exp(dist * (-2.0 / D))
        chosen = lax.dynamic_slice_in_dim(tile_pairs, index * block_tiles, block_tiles, 0).astype(jnp.float32)
        values = values.reshape(block_tiles, TILE, tiles, TILE) * chosen[:, None, :, None]
        kernel = values.reshape(block_rows, total).astype(jnp.bfloat16)
        return jnp.dot(kernel, panel, preferred_element_type=jnp.float32)

    result = lax.map(one_block, jnp.arange(total // block_rows, dtype=jnp.int32))
    return result.reshape(total, P_SIZE)
```

```python
import jax
import jax.numpy as jnp
from jax import lax
from jax.experimental import pallas as pl
from jax.experimental.pallas import tpu as pltpu
from jax.sharding import PartitionSpec as P

D = 64
PW = 16
TILE = 128
BLK = 384
NX, NY, NZ = 4, 4, 8
PLANE = NX * NY * 2
CT = 3 * PLANE
RT = 3 * NZ
PAIRS = RT // 2
BIG = 9984.0
F32, BF16 = jnp.float32, jnp.bfloat16
MESH = pl.DeviceIdType.MESH
VMEM = pl.BlockSpec(memory_space=pltpu.VMEM)
SMEM = pl.BlockSpec(memory_space=pltpu.SMEM)


def place():
    row, col = lax.axis_index("row"), lax.axis_index("col")
    x = (col // 4) * 2 + row // 16
    return x, col % 4, (row // 2) % 8, row % 2


def device(x, y, z, core):
    return ((x % 2) * 16 + z * 2 + core, (x // 2) * 4 + y)


def slot_of(x, y, core):
    return (x % 2) * 16 + core * 8 + (x // 2) * 4 + y


def iota(shape, dim):
    return lax.broadcasted_iota(jnp.int32, shape, dim)


def norm_parts(x_t):
    floats = x_t.astype(F32)
    n = jnp.sum(floats * floats, axis=0, keepdims=True) * (-1.0 / 32.0)
    hi = n.astype(BF16).astype(F32)
    rest = n - hi
    mid = rest.astype(BF16).astype(F32)
    return hi, mid, rest - mid


def mix(rows, first, hi, mid, lo, other):
    one = jnp.where((rows >= other) & (rows < other + 3), 1.0, 0.0)
    return jnp.where(rows == first, hi, jnp.where(rows == first + 1, mid, jnp.where(rows == first + 2, lo, one)))


def lists_of(m, list_ref, info_ref):
    gram = lax.dot_general(m, m, (((1,), (1,)), ((), ())), preferred_element_type=F32)
    sub, lane = iota((RT, RT), 0), iota((RT, RT), 1)
    eye = sub == lane
    n_col = jnp.sum(m, axis=1, keepdims=True)
    n_row = jnp.sum(jnp.where(eye, gram, 0.0), axis=0, keepdims=True)
    apart = n_col + n_row - 2.0 * gram

    def key_of(overlap, apart0, ids, axis):
        score = jnp.where(apart0 > 0.5, overlap * 32.0 - ids.astype(F32), -1e6)
        return score == jnp.max(score, axis=axis, keepdims=True)

    o_row, a_row = gram[0:1, :], apart[0:1, :]
    o_col, a_col = gram[:, 0:1], apart[:, 0:1]
    e_row = key_of(o_row, a_row, lane[0:1, :], 1)
    e_col = key_of(o_col, a_col, sub[:, 0:1], 0)
    p_col = jnp.sum(jnp.where(e_row, gram, 0.0), axis=1, keepdims=True)
    p_row = jnp.sum(jnp.where(e_col, gram, 0.0), axis=0, keepdims=True)

    def order(o, p, a):
        return jnp.where(a < 0.5, 0.0, jnp.where(p > o, 1e4 - o, 2e4 + o))

    k_row, k_col = order(o_row, p_row, a_row), order(o_col, p_col, a_col)
    before = (k_col < k_row) | ((k_col == k_row) & (sub < lane))
    rank = jnp.sum(before.astype(F32), axis=0, keepdims=True)
    pair = iota((16, RT), 0).astype(F32)
    even = jnp.where(rank == 2.0 * pair, 1.0, 0.0)
    odd = jnp.where(rank == 2.0 * pair + 1.0, 1.0, 0.0)
    both = jnp.maximum(
        jnp.dot(even, m, preferred_element_type=F32), jnp.dot(odd, m, preferred_element_type=F32)
    )
    tri = jnp.where(iota((128, 128), 0) < iota((128, 128), 1), 1.0, 0.0)
    pos = jnp.dot(both, tri, preferred_element_type=F32)
    count = jnp.sum(both, axis=1, keepdims=True)
    where = jnp.where(both > 0.5, pos, -1.0)
    ids = iota((16, 128), 1)
    k = iota((128, 128), 0).astype(F32)
    prow = iota((16, 128), 0)
    total = jnp.where(ids.astype(F32) >= count, float(CT), 0.0)
    for p in range(PAIRS):
        hit = jnp.where(where[p : p + 1, :] == k, 1.0, 0.0)
        got = lax.dot_general(ids.astype(F32), hit, (((1,), (1,)), ((), ())), preferred_element_type=F32)
        total = total + jnp.where(prow == p, got, 0.0)
    list_ref[...] = total.astype(jnp.int32)
    t = iota((16, RT), 1).astype(F32)
    first = jnp.sum(even * t, axis=1, keepdims=True)
    second = jnp.sum(odd * t, axis=1, keepdims=True)
    info = jnp.where(ids == 0, first, jnp.where(ids == 1, second, jnp.where(ids == 2, count, 0.0)))
    info_ref[...] = info.astype(jnp.int32)


def gather_kernel(
    pts, pan, tp, xj, vj, xi, lists, info, own, colbuf, rowbuf, mask, psend, precv, fsend, frecv, zsend, zrecv
):
    x, y, z, core = place()
    c = (x // 2) * 4 + y
    me = slot_of(x, y, core)

    def peer(o):
        return (x + o // 4) % 4, (y + o % 4) % 4

    barrier = pltpu.get_barrier_semaphore()
    for o in range(1, 16):
        px, py = peer(o)
        pl.semaphore_signal(barrier, inc=1, device_id=device(px, py, z, core), device_id_type=MESH)
    for o in range(1, NZ):
        pl.semaphore_signal(barrier, inc=1, device_id=device(x, y, (z + o) % NZ, core), device_id_type=MESH)
    pl.semaphore_signal(barrier, inc=1, device_id=device(x, y, z, 1 - core), device_id_type=MESH)

    own[0:D, :] = pts[...].astype(F32).T.astype(BF16)
    own[D : D + PW, :] = pan[...].astype(F32).T.astype(BF16)
    r, t = iota((16, 24), 0), iota((16, 24), 1)
    flags = tp[...].astype(F32)
    pick0 = jnp.where((r < 3) & (t == 3 * c + r), 1.0, 0.0)
    pick1 = jnp.where((r >= 3) & (r < 6) & (t == 3 * c + r - 3), 1.0, 0.0)
    own[D + PW : D + PW + 16, :] = (
        jnp.dot(pick0, flags[:, :BLK], preferred_element_type=F32)
        + jnp.dot(pick1, flags[:, BLK:], preferred_element_type=F32)
    ).astype(BF16)
    pl.semaphore_wait(barrier, 15 + NZ - 1 + 1)

    def plane_copy(o):
        px, py = peer(o)
        return pltpu.make_async_remote_copy(
            src_ref=own.at[0 : D + PW],
            dst_ref=colbuf.at[me],
            send_sem=psend.at[o],
            recv_sem=precv.at[me],
            device_id=device(px, py, z, core),
            device_id_type=MESH,
        )

    def z_copy(o):
        return pltpu.make_async_remote_copy(
            src_ref=own,
            dst_ref=rowbuf.at[z],
            send_sem=zsend.at[o],
            recv_sem=zrecv.at[z],
            device_id=device(x, y, (z + o) % NZ, core),
            device_id_type=MESH,
        )

    def fwd_copy(slot, src):
        return pltpu.make_async_remote_copy(
            src_ref=src,
            dst_ref=colbuf.at[slot],
            send_sem=fsend.at[slot],
            recv_sem=frecv.at[slot],
            device_id=device(x, y, z, 1 - core),
            device_id_type=MESH,
        )

    near = (1, 3, 4, 12, 2, 8, 5, 7, 13, 15, 6, 14, 9, 11, 10)
    z_near = (1, 7, 2, 6, 3, 5, 4)
    for o in z_near:
        z_copy(o).start()
    for o in near:
        plane_copy(o).start()
    fwd_copy(me, own.at[0 : D + PW]).start()

    rowbuf[z] = own[...]
    colbuf[me] = own[0 : D + PW, :]
    xj[CT] = jnp.zeros((TILE, TILE), BF16)
    vj[CT] = jnp.zeros((PW, TILE), BF16)

    lane = iota((BLK, 128), 1)
    pos = iota((BLK, 128), 0) - 48 * z
    shift0 = jnp.where((lane < 48) & (pos == lane), 1.0, 0.0)
    shift1 = jnp.where((lane >= 48) & (lane < 96) & (pos == lane - 48), 1.0, 0.0)
    mask[...] = jnp.zeros((RT, 128), F32)
    row64 = iota((64, TILE), 0)
    for o in (0,) + z_near:
        zz = (z + o) % NZ
        if o:
            pltpu.make_async_remote_copy(
                src_ref=own,
                dst_ref=rowbuf.at[zz],
                send_sem=zsend.at[o],
                recv_sem=zrecv.at[zz],
                device_id=device(x, y, zz, core),
                device_id_type=MESH,
            ).wait_recv()
        block = rowbuf[zz]
        hi, mid, lo = norm_parts(block[0:D, :])
        for q in range(3):
            at = slice(q * TILE, (q + 1) * TILE)
            tail = mix(row64, 0, hi[:, at], mid[:, at], lo[:, at], 3)
            tail = jnp.where(row64 == 8 + 3 * zz + q, 1.0, tail)
            xi[3 * zz + q, 0:D, :] = block[0:D, at] * jnp.bfloat16(1.0 / 16.0)
            xi[3 * zz + q, D:128, :] = tail.astype(BF16)
        flag = block[D + PW :, :].astype(F32)
        got0 = jnp.dot(flag, shift0, preferred_element_type=F32)
        got1 = jnp.dot(flag, shift1, preferred_element_type=F32)
        mine = iota((RT, 16), 0) - 3 * zz
        src = iota((RT, 16), 1)
        put0 = jnp.where((mine >= 0) & (mine < 3) & (src == mine), 1.0, 0.0)
        put1 = jnp.where((mine >= 0) & (mine < 3) & (src == mine + 3), 1.0, 0.0)
        mask[...] += jnp.dot(put0, got0, preferred_element_type=F32) + jnp.dot(
            put1, got1, preferred_element_type=F32
        )
    lists_of(mask[...], lists, info)

    def column(slot):
        block = colbuf[slot]
        hi, mid, lo = norm_parts(block[0:D, :])
        lanes = iota((RT, 128), 1)
        for q in range(3):
            at = slice(q * TILE, (q + 1) * TILE)
            tail = mix(row64[0:8], 3, hi[:, at], mid[:, at], lo[:, at], 0)
            on = jnp.sum(jnp.where(lanes == 3 * slot + q, mask[...], 0.0), axis=1, keepdims=True)
            off = jnp.broadcast_to((on - 1.0) * BIG, (RT, TILE))
            feats = jnp.concatenate(
                [block[0:D, at].astype(F32), tail, off, jnp.zeros((128 - D - 8 - RT, TILE), F32)], axis=0
            )
            xj[3 * slot + q] = feats.T.astype(BF16)
            vj[3 * slot + q] = block[D:, at]

    column(me)

    def arrive(o):
        px, py = peer(o)
        slot = slot_of(px, py, core)
        pltpu.make_async_remote_copy(
            src_ref=own.at[0 : D + PW],
            dst_ref=colbuf.at[slot],
            send_sem=psend.at[o],
            recv_sem=precv.at[slot],
            device_id=device(px, py, z, core),
            device_id_type=MESH,
        ).wait_recv()
        fwd_copy(slot, colbuf.at[slot]).start()
        return slot

    for o in near:
        column(arrive(o))
    for o in (0,) + near:
        px, py = peer(o)
        slot = slot_of(px, py, 1 - core)
        fwd_copy(slot, colbuf.at[slot]).wait_recv()
        column(slot)
    for o in z_near:
        z_copy(o).wait_send()
    for o in near:
        plane_copy(o).wait_send()
    for o in (0,) + near:
        px, py = peer(o)
        slot = slot_of(px, py, core)
        fwd_copy(slot, colbuf.at[slot]).wait_send()


JT = 4
SUB = 4


def apply_kernel(lists, info, xj, vj, xi, out, *held):
    out[...] = jnp.zeros_like(out)

    def compute(p, k, held_ref):
        w = jnp.concatenate([xi[info[p, 0]], xi[info[p, 1]]], axis=1)
        a = jnp.concatenate([xj[lists[p, k + q]] for q in range(JT)], axis=0)
        s = jnp.dot(a, w, preferred_element_type=F32)
        held_ref[...] = jnp.exp(jnp.minimum(s, 0.0)).astype(BF16)

    def apply(p, k, held_ref):
        v = jnp.concatenate([vj[lists[p, k + q]] for q in range(JT)], axis=1)
        r = jnp.dot(v, held_ref[...], preferred_element_type=F32)
        a, b = info[p, 0], info[p, 1]
        out[a] += r[:, :TILE]
        out[b] += r[:, TILE:]

    def following(p, k):
        end = k + JT >= info[p, 2]
        last = p == PAIRS - 1
        k = jnp.where(end, jnp.where(last, 100, 0), k + JT)
        return jnp.where(end & ~last, p + 1, p), k

    total = sum(jnp.maximum((info[p, 2] + JT - 1) // JT, 1) for p in range(PAIRS))
    zero = jnp.int32(0)
    compute(zero, zero, held[SUB - 1])

    def step(_, at):
        for u in range(SUB):
            nxt = following(*at)
            compute(*nxt, held[u])
            apply(*at, held[u - 1])
            at = nxt
        return at

    lax.fori_loop(0, (total + SUB - 1) // SUB, step, (zero, zero))


def reduce_kernel(part, out, got, send, recv):
    x, y, z, core = place()
    barrier = pltpu.get_barrier_semaphore()
    for o in range(1, NZ):
        pl.semaphore_signal(barrier, inc=1, device_id=device(x, y, (z + o) % NZ, core), device_id_type=MESH)
    pl.semaphore_wait(barrier, NZ - 1)

    def copy(o, slot):
        to = (z + o) % NZ
        return pltpu.make_async_remote_copy(
            src_ref=part.at[pl.ds(3 * to, 3)],
            dst_ref=got.at[slot],
            send_sem=send.at[o],
            recv_sem=recv.at[slot],
            device_id=device(x, y, to, core),
            device_id_type=MESH,
        )

    for o in (4, 3, 5, 2, 6, 1, 7):
        copy(o, z).start()
    total = [part[3 * z + q] for q in range(3)]
    for o in (1, 7, 2, 6, 3, 5, 4):
        zz = (z + o) % NZ
        copy(o, zz).wait_recv()
        total = [total[q] + got[zz, q] for q in range(3)]
    for q in range(3):
        out[q * TILE : (q + 1) * TILE, :] = total[q].T
    for o in range(1, NZ):
        copy(o, z).wait_send()


def local(points, panel, tile_pairs):
    shape = jax.ShapeDtypeStruct
    dma = pltpu.SemaphoreType.DMA
    xj, vj, xi, lists, info = pl.pallas_call(
        gather_kernel,
        out_shape=(
            shape((CT + 1, TILE, TILE), BF16),
            shape((CT + 1, PW, TILE), BF16),
            shape((RT, TILE, TILE), BF16),
            shape((16, 128), jnp.int32),
            shape((16, 128), jnp.int32),
        ),
        in_specs=[VMEM] * 3,
        out_specs=[VMEM] * 5,
        scratch_shapes=[
            pltpu.VMEM((D + PW + 16, BLK), BF16),
            pltpu.VMEM((PLANE, D + PW, BLK), BF16),
            pltpu.VMEM((NZ, D + PW + 16, BLK), BF16),
            pltpu.VMEM((RT, 128), F32),
            dma((16,)),
            dma((PLANE,)),
            dma((PLANE,)),
            dma((PLANE,)),
            dma((NZ,)),
            dma((NZ,)),
        ],
        compiler_params=pltpu.CompilerParams(
            collective_id=0, has_side_effects=True, vmem_limit_bytes=40 * 2**20
        ),
        name="gather",
    )(points, panel, tile_pairs)
    part = pl.pallas_call(
        apply_kernel,
        out_shape=shape((RT, PW, TILE), F32),
        in_specs=[SMEM, SMEM, VMEM, VMEM, VMEM],
        out_specs=VMEM,
        scratch_shapes=[pltpu.VMEM((JT * TILE, 2 * TILE), BF16)] * SUB,
        compiler_params=pltpu.CompilerParams(vmem_limit_bytes=40 * 2**20),
        name="apply",
    )(lists, info, xj, vj, xi)
    return pl.pallas_call(
        reduce_kernel,
        out_shape=shape((BLK, PW), F32),
        in_specs=[VMEM],
        out_specs=VMEM,
        scratch_shapes=[pltpu.VMEM((NZ, 3, PW, TILE), F32), dma((NZ,)), dma((NZ,))],
        compiler_params=pltpu.CompilerParams(
            collective_id=1, has_side_effects=True, vmem_limit_bytes=40 * 2**20
        ),
        name="reduce",
    )(part)


def solution(mesh):
    in_specs = (P(("row", "col"), None), P(("row", "col"), None), P("row", None))
    out_specs = P(("row", "col"), None)
    return jax.shard_map(local, mesh=mesh, in_specs=in_specs, out_specs=out_specs, check_vma=False)
```

```python
import jax
import jax.numpy as jnp
from jax import lax
from jax.experimental import pallas as pl
from jax.experimental.pallas import tpu as pltpu
from jax.sharding import PartitionSpec as P

D = 64
PW = 16
TILE = 128
BLK = 384
NX, NY, NZ = 4, 4, 8
PLANE = NX * NY * 2
CT = 3 * PLANE
RT = 3 * NZ
PAIRS = RT // 2
BIG = 9984.0
F32, BF16 = jnp.float32, jnp.bfloat16
MESH = pl.DeviceIdType.MESH
VMEM = pl.BlockSpec(memory_space=pltpu.VMEM)
SMEM = pl.BlockSpec(memory_space=pltpu.SMEM)


def place():
    row, col = lax.axis_index("row"), lax.axis_index("col")
    x = (col // 4) * 2 + row // 16
    return x, col % 4, (row // 2) % 8, row % 2


def device(x, y, z, core):
    return ((x % 2) * 16 + z * 2 + core, (x // 2) * 4 + y)


def slot_of(x, y, core):
    return (x % 2) * 16 + core * 8 + (x // 2) * 4 + y


def iota(shape, dim):
    return lax.broadcasted_iota(jnp.int32, shape, dim)


def norm_parts(x_t):
    floats = x_t.astype(F32)
    n = jnp.sum(floats * floats, axis=0, keepdims=True) * (-1.0 / 32.0)
    hi = n.astype(BF16).astype(F32)
    rest = n - hi
    mid = rest.astype(BF16).astype(F32)
    return hi, mid, rest - mid


def mix(rows, first, hi, mid, lo, other):
    one = jnp.where((rows >= other) & (rows < other + 3), 1.0, 0.0)
    return jnp.where(rows == first, hi, jnp.where(rows == first + 1, mid, jnp.where(rows == first + 2, lo, one)))


def lists_of(m, list_ref, info_ref):
    gram = lax.dot_general(m, m, (((1,), (1,)), ((), ())), preferred_element_type=F32)
    sub, lane = iota((RT, RT), 0), iota((RT, RT), 1)
    eye = sub == lane
    n_col = jnp.sum(m, axis=1, keepdims=True)
    n_row = jnp.sum(jnp.where(eye, gram, 0.0), axis=0, keepdims=True)
    apart = n_col + n_row - 2.0 * gram

    def key_of(overlap, apart0, ids, axis):
        score = jnp.where(apart0 > 0.5, overlap * 32.0 - ids.astype(F32), -1e6)
        return score == jnp.max(score, axis=axis, keepdims=True)

    o_row, a_row = gram[0:1, :], apart[0:1, :]
    o_col, a_col = gram[:, 0:1], apart[:, 0:1]
    e_row = key_of(o_row, a_row, lane[0:1, :], 1)
    e_col = key_of(o_col, a_col, sub[:, 0:1], 0)
    p_col = jnp.sum(jnp.where(e_row, gram, 0.0), axis=1, keepdims=True)
    p_row = jnp.sum(jnp.where(e_col, gram, 0.0), axis=0, keepdims=True)

    def order(o, p, a):
        return jnp.where(a < 0.5, 0.0, jnp.where(p > o, 1e4 - o, 2e4 + o))

    k_row, k_col = order(o_row, p_row, a_row), order(o_col, p_col, a_col)
    before = (k_col < k_row) | ((k_col == k_row) & (sub < lane))
    rank = jnp.sum(before.astype(F32), axis=0, keepdims=True)
    pair = iota((16, RT), 0).astype(F32)
    even = jnp.where(rank == 2.0 * pair, 1.0, 0.0)
    odd = jnp.where(rank == 2.0 * pair + 1.0, 1.0, 0.0)
    both = jnp.maximum(
        jnp.dot(even, m, preferred_element_type=F32), jnp.dot(odd, m, preferred_element_type=F32)
    )
    tri = jnp.where(iota((128, 128), 0) < iota((128, 128), 1), 1.0, 0.0)
    pos = jnp.dot(both, tri, preferred_element_type=F32)
    count = jnp.sum(both, axis=1, keepdims=True)
    where = jnp.where(both > 0.5, pos, -1.0)
    ids = iota((16, 128), 1)
    k = iota((128, 128), 0).astype(F32)
    prow = iota((16, 128), 0)
    total = jnp.where(ids.astype(F32) >= count, float(CT), 0.0)
    for p in range(PAIRS):
        hit = jnp.where(where[p : p + 1, :] == k, 1.0, 0.0)
        got = lax.dot_general(ids.astype(F32), hit, (((1,), (1,)), ((), ())), preferred_element_type=F32)
        total = total + jnp.where(prow == p, got, 0.0)
    list_ref[...] = total.astype(jnp.int32)
    t = iota((16, RT), 1).astype(F32)
    first = jnp.sum(even * t, axis=1, keepdims=True)
    second = jnp.sum(odd * t, axis=1, keepdims=True)
    info = jnp.where(ids == 0, first, jnp.where(ids == 1, second, jnp.where(ids == 2, count, 0.0)))
    info_ref[...] = info.astype(jnp.int32)


def gather_kernel(
    pts, pan, tp, xj, vj, xi, lists, info,
    own, colbuf, rowbuf, flags, flagbuf, mask, psend, precv, fsend, frecv, zsend, zrecv, gsend, grecv,
):
    x, y, z, core = place()
    c = (x // 2) * 4 + y
    me = slot_of(x, y, core)

    def at(d):
        return (x + d[0]) % 4, (y + d[1]) % 4

    def slot(d, which=core):
        return slot_of(*at(d), which)

    barrier = pltpu.get_barrier_semaphore()
    for o in range(1, 16):
        pl.semaphore_signal(barrier, inc=1, device_id=device(*at((o // 4, o % 4)), z, core), device_id_type=MESH)
    for o in range(1, NZ):
        pl.semaphore_signal(barrier, inc=1, device_id=device(x, y, (z + o) % NZ, core), device_id_type=MESH)
    pl.semaphore_signal(barrier, inc=1, device_id=device(x, y, z, 1 - core), device_id_type=MESH)

    own[0:D, :] = pts[...]
    own[D:, :] = pan[...]
    r, t = iota((16, 24), 0), iota((16, 24), 1)
    pick = jnp.where((r < 3) & (t == 3 * c + r), 1.0, 0.0)
    rows = jnp.dot(pick, tp[...].astype(F32), preferred_element_type=F32)
    for zz in range(NZ):
        low = rows[:, 48 * zz : 48 * zz + 48]
        high = rows[:, BLK + 48 * zz : BLK + 48 * zz + 48]
        flags[zz] = jnp.concatenate([low, high, jnp.zeros((16, 32), F32)], axis=1).astype(BF16)
    pl.semaphore_wait(barrier, 15 + NZ - 1 + 1)

    def remote(src, dst, send, recv, to):
        return pltpu.make_async_remote_copy(
            src_ref=src, dst_ref=dst, send_sem=send, recv_sem=recv, device_id=to, device_id_type=MESH
        )

    sent = []

    def start(copy):
        copy.start()
        sent.append(copy)

    def plane(src, s, d, i):
        start(remote(src, colbuf.at[s], psend.at[i], precv.at[s], device(*at(d), z, core)))

    def line(src, s, o, i):
        start(remote(src, rowbuf.at[s], zsend.at[i], zrecv.at[s], device(x, y, (z + o) % NZ, core)))

    sibling = device(x, y, z, 1 - core)

    def forward(src, s):
        start(remote(src, colbuf.at[s], fsend.at[s], frecv.at[s], sibling))

    def from_plane(s):
        remote(own, colbuf.at[s], psend.at[0], precv.at[s], sibling).wait_recv()

    def from_line(s):
        remote(own, rowbuf.at[s], zsend.at[0], zrecv.at[s], sibling).wait_recv()

    def from_sibling(s):
        remote(own, colbuf.at[s], fsend.at[s], frecv.at[s], sibling).wait_recv()

    for o in (4, 3, 5, 2, 6, 1, 7):
        to = (z + o) % NZ
        start(remote(flags.at[to], flagbuf.at[z], gsend.at[o], grecv.at[z], device(x, y, to, core)))
    near = ((1, 0), (3, 0), (0, 1), (0, 3), (1, 1), (1, 3), (3, 1), (3, 3))
    two = ((2, 0), (0, 2))
    far = ((2, 1), (2, 3), (1, 2), (3, 2), (2, 2))
    for i, o in enumerate((2, 6, 1, 7)):
        line(own, z, o, i)
    for i, d in enumerate(two + near):
        plane(own, me, d, i)
    forward(own, me)

    row64 = iota((64, TILE), 0)

    def row(zz, block):
        hi, mid, lo = norm_parts(block[0:D, :])
        for q in range(3):
            cut = slice(q * TILE, (q + 1) * TILE)
            tail = mix(row64, 0, hi[:, cut], mid[:, cut], lo[:, cut], 3)
            tail = jnp.where(row64 == 8 + 3 * zz + q, 1.0, tail)
            xi[3 * zz + q, 0:D, :] = block[0:D, cut] * jnp.bfloat16(1.0 / 16.0)
            xi[3 * zz + q, D:128, :] = tail.astype(BF16)

    lanes = iota((RT, 128), 1)

    def column(s, block):
        hi, mid, lo = norm_parts(block[0:D, :])
        for q in range(3):
            cut = slice(q * TILE, (q + 1) * TILE)
            tail = mix(row64[0:8], 3, hi[:, cut], mid[:, cut], lo[:, cut], 0)
            on = jnp.sum(jnp.where(lanes == 3 * s + q, mask[...], 0.0), axis=1, keepdims=True)
            off = jnp.broadcast_to((on - 1.0) * BIG, (RT, TILE))
            feats = jnp.concatenate(
                [block[0:D, cut].astype(F32), tail, off, jnp.zeros((128 - D - 8 - RT, TILE), F32)], axis=0
            )
            xj[3 * s + q] = feats.T.astype(BF16)
            vj[3 * s + q] = block[D:, cut]

    xj[CT] = jnp.zeros((TILE, TILE), BF16)
    vj[CT] = jnp.zeros((PW, TILE), BF16)
    row(z, own[...])

    s = slot((2, 0))
    from_plane(s)
    plane(colbuf.at[s], s, (0, 1), 10)
    plane(colbuf.at[s], s, (0, 3), 11)
    s = slot((0, 2))
    from_plane(s)
    plane(colbuf.at[s], s, (1, 0), 12)
    plane(colbuf.at[s], s, (3, 0), 13)
    s = slot((2 * (1 - core), 2 * core))
    plane(colbuf.at[s], s, (2 * core, 2 * (1 - core)), 14)
    s = (z + 6) % NZ
    from_line(s)
    line(rowbuf.at[s], s, 1, 4)
    line(rowbuf.at[s], s, 2, 5)
    s = (z + 2) % NZ
    from_line(s)
    line(rowbuf.at[s], s, 7, 6)
    for d in two:
        forward(colbuf.at[slot(d)], slot(d))

    for o in range(1, NZ):
        zz = (z + o) % NZ
        remote(flags.at[0], flagbuf.at[zz], gsend.at[o], grecv.at[zz], sibling).wait_recv()
    flagbuf[z] = flags[z]
    for zz in range(NZ):
        mask[3 * zz : 3 * zz + 3, :] = flagbuf[zz].astype(F32)[0:3, :]
    lists_of(mask[...], lists, info)
    column(me, own[...])
    for d in two:
        column(slot(d), colbuf[slot(d)])
    for d in near:
        from_plane(slot(d))
        forward(colbuf.at[slot(d)], slot(d))
        column(slot(d), colbuf[slot(d)])
    for o in (2, 6, 1, 7):
        zz = (z + o) % NZ
        if o in (1, 7):
            from_line(zz)
        row(zz, rowbuf[zz])
    first = ((0, 0),) + two + near
    for d in first[:3]:
        s = slot(d, 1 - core)
        from_sibling(s)
        column(s, colbuf[s])
    for d in far:
        from_plane(slot(d))
        forward(colbuf.at[slot(d)], slot(d))
    for d in far:
        column(slot(d), colbuf[slot(d)])
    for d in first[3:]:
        s = slot(d, 1 - core)
        from_sibling(s)
        column(s, colbuf[s])
    for o in (3, 5, 4):
        zz = (z + o) % NZ
        from_line(zz)
        row(zz, rowbuf[zz])
    for d in far:
        s = slot(d, 1 - core)
        from_sibling(s)
        column(s, colbuf[s])
    for copy in sent:
        copy.wait_send()


JT = 8
SUB = 8


def apply_kernel(lists, info, xj, vj, xi, out, *held):
    out[...] = jnp.zeros_like(out)

    def weights(p):
        return jnp.concatenate([xi[info[p, 0]], xi[info[p, 1]]], axis=1)

    def compute(p, k, q, w, held_ref):
        s = jnp.dot(xj[lists[p, k + q]], w, preferred_element_type=F32)
        held_ref[q * TILE : (q + 1) * TILE, :] = jnp.exp(jnp.minimum(s, 0.0)).astype(BF16)

    def apply(p, k, q, held_ref):
        v = jnp.concatenate([vj[lists[p, k + q]], vj[lists[p, k + q + 1]]], axis=1)
        return jnp.dot(v, held_ref[q * TILE : (q + 2) * TILE, :], preferred_element_type=F32)

    def following(p, k):
        end = k + JT >= info[p, 2]
        last = p == PAIRS - 1
        k = jnp.where(end, jnp.where(last, 100, 0), k + JT)
        return jnp.where(end & ~last, p + 1, p), k

    total = sum(jnp.maximum((info[p, 2] + JT - 1) // JT, 1) for p in range(PAIRS))
    zero = jnp.int32(0)
    w = weights(zero)
    for q in range(JT):
        compute(zero, zero, q, w, held[SUB - 1])

    def step(_, at):
        for u in range(SUB):
            nxt = following(*at)
            w = weights(nxt[0])
            r = None
            for q in range(JT):
                compute(*nxt, q, w, held[u])
                if q % 2 == 0:
                    part = apply(*at, q, held[u - 1])
                    r = part if r is None else r + part
            a, b = info[at[0], 0], info[at[0], 1]
            out[a] += r[:, :TILE]
            out[b] += r[:, TILE:]
            at = nxt
        return at

    lax.fori_loop(0, (total + SUB - 1) // SUB, step, (zero, zero))


def reduce_kernel(part, out, got, send, recv):
    x, y, z, core = place()
    barrier = pltpu.get_barrier_semaphore()
    for o in range(1, NZ):
        pl.semaphore_signal(barrier, inc=1, device_id=device(x, y, (z + o) % NZ, core), device_id_type=MESH)
    pl.semaphore_wait(barrier, NZ - 1)

    def copy(o, slot):
        to = (z + o) % NZ
        return pltpu.make_async_remote_copy(
            src_ref=part.at[pl.ds(3 * to, 3)],
            dst_ref=got.at[slot],
            send_sem=send.at[o],
            recv_sem=recv.at[slot],
            device_id=device(x, y, to, core),
            device_id_type=MESH,
        )

    for o in (4, 3, 5, 2, 6, 1, 7):
        copy(o, z).start()
    total = [part[3 * z + q] for q in range(3)]
    for o in (1, 7, 2, 6, 3, 5, 4):
        zz = (z + o) % NZ
        copy(o, zz).wait_recv()
        total = [total[q] + got[zz, q] for q in range(3)]
    for q in range(3):
        out[:, q * TILE : (q + 1) * TILE] = total[q]
    for o in range(1, NZ):
        copy(o, z).wait_send()


def local(points, panel, tile_pairs):
    shape = jax.ShapeDtypeStruct
    dma = pltpu.SemaphoreType.DMA
    xj, vj, xi, lists, info = pl.pallas_call(
        gather_kernel,
        out_shape=(
            shape((CT + 1, TILE, TILE), BF16),
            shape((CT + 1, PW, TILE), BF16),
            shape((RT, TILE, TILE), BF16),
            shape((16, 128), jnp.int32),
            shape((16, 128), jnp.int32),
        ),
        in_specs=[VMEM] * 3,
        out_specs=[VMEM] * 5,
        scratch_shapes=[
            pltpu.VMEM((D + PW, BLK), BF16),
            pltpu.VMEM((PLANE, D + PW, BLK), BF16),
            pltpu.VMEM((NZ, D + PW, BLK), BF16),
            pltpu.VMEM((NZ, 16, 128), BF16),
            pltpu.VMEM((NZ, 16, 128), BF16),
            pltpu.VMEM((RT, 128), F32),
            dma((16,)),
            dma((PLANE,)),
            dma((PLANE,)),
            dma((PLANE,)),
            dma((NZ,)),
            dma((NZ,)),
            dma((NZ,)),
            dma((NZ,)),
        ],
        compiler_params=pltpu.CompilerParams(
            collective_id=0, has_side_effects=True, vmem_limit_bytes=40 * 2**20
        ),
        name="gather",
    )(points.T, panel.T, tile_pairs)
    part = pl.pallas_call(
        apply_kernel,
        out_shape=shape((RT, PW, TILE), F32),
        in_specs=[SMEM, SMEM, VMEM, VMEM, VMEM],
        out_specs=VMEM,
        scratch_shapes=[pltpu.VMEM((JT * TILE, 2 * TILE), BF16)] * SUB,
        compiler_params=pltpu.CompilerParams(vmem_limit_bytes=40 * 2**20),
        name="apply",
    )(lists, info, xj, vj, xi)
    return pl.pallas_call(
        reduce_kernel,
        out_shape=shape((PW, BLK), F32),
        in_specs=[VMEM],
        out_specs=VMEM,
        scratch_shapes=[pltpu.VMEM((NZ, 3, PW, TILE), F32), dma((NZ,)), dma((NZ,))],
        compiler_params=pltpu.CompilerParams(
            collective_id=1, has_side_effects=True, vmem_limit_bytes=40 * 2**20
        ),
        name="reduce",
    )(part).T


def solution(mesh):
    in_specs = (P(("row", "col"), None), P(("row", "col"), None), P("row", None))
    out_specs = P(("row", "col"), None)
    return jax.shard_map(local, mesh=mesh, in_specs=in_specs, out_specs=out_specs, check_vma=False)
```

```python
import jax
import jax.numpy as jnp
from jax import lax
from jax.experimental import pallas as pl
from jax.experimental.pallas import tpu as pltpu
from jax.sharding import PartitionSpec as P

D = 64
PW = 16
TILE = 128
BLK = 384
NX, NY, NZ = 4, 4, 8
PLANE = NX * NY * 2
CT = 3 * PLANE
RT = 3 * NZ
PAIRS = (RT - 2) // 2
BIG = 9984.0
F32, BF16 = jnp.float32, jnp.bfloat16
MESH = pl.DeviceIdType.MESH
VMEM = pl.BlockSpec(memory_space=pltpu.VMEM)
HBM = pl.BlockSpec(memory_space=pltpu.HBM)
SMEM = pl.BlockSpec(memory_space=pltpu.SMEM)


def place():
    row, col = lax.axis_index("row"), lax.axis_index("col")
    x = (col // 4) * 2 + row // 16
    return x, col % 4, (row // 2) % 8, row % 2


def device(x, y, z, core):
    return ((x % 2) * 16 + z * 2 + core, (x // 2) * 4 + y)


def slot_of(x, y, core):
    return (x % 2) * 16 + core * 8 + (x // 2) * 4 + y


def iota(shape, dim):
    return lax.broadcasted_iota(jnp.int32, shape, dim)


def norm_parts(x_t):
    floats = x_t.astype(F32)
    n = jnp.sum(floats * floats, axis=0, keepdims=True) * (-1.0 / 32.0)
    hi = n.astype(BF16).astype(F32)
    rest = n - hi
    mid = rest.astype(BF16).astype(F32)
    return hi, mid, rest - mid


def mix(rows, first, hi, mid, lo, other):
    one = jnp.where((rows >= other) & (rows < other + 3), 1.0, 0.0)
    return jnp.where(rows == first, hi, jnp.where(rows == first + 1, mid, jnp.where(rows == first + 2, lo, one)))


def lists_of(m, z, list_ref, info_ref):
    gram = lax.dot_general(m, m, (((1,), (1,)), ((), ())), preferred_element_type=F32)
    sub, lane = iota((RT, RT), 0), iota((RT, RT), 1)
    eye = sub == lane
    n_col = jnp.sum(m, axis=1, keepdims=True)
    n_row = jnp.sum(jnp.where(eye, gram, 0.0), axis=0, keepdims=True)
    apart = n_col + n_row - 2.0 * gram

    def key_of(overlap, apart0, ids, axis):
        score = jnp.where(apart0 > 0.5, overlap * 32.0 - ids.astype(F32), -1e6)
        return score == jnp.max(score, axis=axis, keepdims=True)

    o_row, a_row = gram[0:1, :], apart[0:1, :]
    o_col, a_col = gram[:, 0:1], apart[:, 0:1]
    e_row = key_of(o_row, a_row, lane[0:1, :], 1)
    e_col = key_of(o_col, a_col, sub[:, 0:1], 0)
    p_col = jnp.sum(jnp.where(e_row, gram, 0.0), axis=1, keepdims=True)
    p_row = jnp.sum(jnp.where(e_col, gram, 0.0), axis=0, keepdims=True)

    def order(o, p, a):
        return jnp.where(a < 0.5, 0.0, jnp.where(p > o, 1e4 - o, 2e4 + o))

    def mine(ids):
        return (ids >= 3 * z) & (ids < 3 * z + 3)

    k_row = jnp.where(mine(lane[0:1, :]), 1e6, order(o_row, p_row, a_row))
    k_col = jnp.where(mine(sub[:, 0:1]), 1e6, order(o_col, p_col, a_col))
    before = (k_col < k_row) | ((k_col == k_row) & (sub < lane))
    rank = jnp.sum(before.astype(F32), axis=0, keepdims=True)
    pair = iota((16, RT), 0).astype(F32)
    even = jnp.where(rank == 2.0 * pair, 1.0, 0.0)
    odd = jnp.where(rank == 2.0 * pair + 1.0, 1.0, 0.0)
    m = jnp.where(mine(iota((RT, 128), 0)), 0.0, m)
    both = jnp.maximum(
        jnp.dot(even, m, preferred_element_type=F32), jnp.dot(odd, m, preferred_element_type=F32)
    )
    tri = jnp.where(iota((128, 128), 0) < iota((128, 128), 1), 1.0, 0.0)
    pos = jnp.dot(both, tri, preferred_element_type=F32)
    count = jnp.sum(both, axis=1, keepdims=True)
    where = jnp.where(both > 0.5, pos, -1.0)
    ids = iota((16, 128), 1)
    k = iota((128, 128), 0).astype(F32)
    prow = iota((16, 128), 0)
    total = jnp.where(ids.astype(F32) >= count, float(CT), 0.0)
    for p in range(PAIRS):
        hit = jnp.where(where[p : p + 1, :] == k, 1.0, 0.0)
        got = lax.dot_general(ids.astype(F32), hit, (((1,), (1,)), ((), ())), preferred_element_type=F32)
        total = total + jnp.where(prow == p, got, 0.0)
    list_ref[...] = total.astype(jnp.int32)
    t = iota((16, RT), 1).astype(F32)
    first = jnp.sum(even * t, axis=1, keepdims=True)
    second = jnp.sum(odd * t, axis=1, keepdims=True)
    info = jnp.where(ids == 0, first, jnp.where(ids == 1, second, jnp.where(ids == 2, count, 0.0)))
    info_ref[...] = info.astype(jnp.int32)


def gather_kernel(
    pts, pan, tp, xj, vj, xi, lists, info,
    own, pairs, colbuf, rowbuf, flags, flagbuf, mask, local, psend, precv, fsend, frecv, zsend, zrecv, gsend, grecv,
):
    x, y, z, core = place()
    c = (x // 2) * 4 + y
    me = slot_of(x, y, core)

    def at(d):
        return (x + d[0]) % 4, (y + d[1]) % 4

    def slot(d, which=core):
        return slot_of(*at(d), which)

    fetch = [
        pltpu.make_async_copy(pts, own.at[0:D], local.at[0]),
        pltpu.make_async_copy(pan, own.at[D : D + PW], local.at[1]),
        pltpu.make_async_copy(tp, pairs, local.at[2]),
    ]
    for copy in fetch:
        copy.start()
    barrier = pltpu.get_barrier_semaphore()
    for o in range(1, 16):
        pl.semaphore_signal(barrier, inc=1, device_id=device(*at((o // 4, o % 4)), z, core), device_id_type=MESH)
    for o in range(1, NZ):
        pl.semaphore_signal(barrier, inc=1, device_id=device(x, y, (z + o) % NZ, core), device_id_type=MESH)
    pl.semaphore_signal(barrier, inc=1, device_id=device(x, y, z, 1 - core), device_id_type=MESH)

    for copy in fetch:
        copy.wait()
    r, t = iota((16, 24), 0), iota((16, 24), 1)
    pick = jnp.where((r < 3) & (t == 3 * c + r), 1.0, 0.0)
    rows = jnp.dot(pick, pairs[...].astype(F32), preferred_element_type=F32)
    for zz in range(NZ):
        low = rows[:, 48 * zz : 48 * zz + 48]
        high = rows[:, BLK + 48 * zz : BLK + 48 * zz + 48]
        flags[zz] = jnp.concatenate([low, high, jnp.zeros((16, 32), F32)], axis=1).astype(BF16)
    pl.semaphore_wait(barrier, 15 + NZ - 1 + 1)

    def remote(src, dst, send, recv, to):
        return pltpu.make_async_remote_copy(
            src_ref=src, dst_ref=dst, send_sem=send, recv_sem=recv, device_id=to, device_id_type=MESH
        )

    sent = []

    def start(copy):
        copy.start()
        sent.append(copy)

    def plane(src, s, d, i):
        start(remote(src, colbuf.at[s], psend.at[i], precv.at[s], device(*at(d), z, core)))

    def line(src, s, o, i):
        start(remote(src, rowbuf.at[s], zsend.at[i], zrecv.at[s], device(x, y, (z + o) % NZ, core)))

    sibling = device(x, y, z, 1 - core)

    def forward(src, s):
        start(remote(src, colbuf.at[s], fsend.at[s], frecv.at[s], sibling))

    def from_plane(s):
        remote(own, colbuf.at[s], psend.at[0], precv.at[s], sibling).wait_recv()

    def from_line(s):
        remote(own, rowbuf.at[s], zsend.at[0], zrecv.at[s], sibling).wait_recv()

    def from_sibling(s):
        remote(own, colbuf.at[s], fsend.at[s], frecv.at[s], sibling).wait_recv()

    for o in (4, 3, 5, 2, 6, 1, 7):
        to = (z + o) % NZ
        start(remote(flags.at[to], flagbuf.at[z], gsend.at[o], grecv.at[z], device(x, y, to, core)))
    near = ((1, 0), (3, 0), (0, 1), (0, 3), (1, 1), (1, 3), (3, 1), (3, 3))
    two = ((2, 0), (0, 2))
    far = ((2, 1), (2, 3), (1, 2), (3, 2), (2, 2))
    for i, o in enumerate((2, 6, 1, 7)):
        line(own, z, o, i)
    for i, d in enumerate(two + near):
        plane(own, me, d, i)
    forward(own, me)

    row64 = iota((64, TILE), 0)

    def row(zz, block):
        hi, mid, lo = norm_parts(block[0:D, :])
        for q in range(3):
            cut = slice(q * TILE, (q + 1) * TILE)
            tail = mix(row64, 0, hi[:, cut], mid[:, cut], lo[:, cut], 3)
            tail = jnp.where(row64 == 8 + 3 * zz + q, 1.0, tail)
            xi[3 * zz + q, 0:D, :] = block[0:D, cut] * jnp.bfloat16(1.0 / 16.0)
            xi[3 * zz + q, D:128, :] = tail.astype(BF16)

    lanes = iota((RT, 128), 1)

    def column(s, block):
        hi, mid, lo = norm_parts(block[0:D, :])
        for q in range(3):
            cut = slice(q * TILE, (q + 1) * TILE)
            tail = mix(row64[0:8], 3, hi[:, cut], mid[:, cut], lo[:, cut], 0)
            on = jnp.sum(jnp.where(lanes == 3 * s + q, mask[...], 0.0), axis=1, keepdims=True)
            off = jnp.broadcast_to((on - 1.0) * BIG, (RT, TILE))
            feats = jnp.concatenate(
                [block[0:D, cut].astype(F32), tail, off, jnp.zeros((128 - D - 8 - RT, TILE), F32)], axis=0
            )
            xj[3 * s + q] = feats.T.astype(BF16)
            vj[3 * s + q] = block[D:, cut]

    xj[CT] = jnp.zeros((TILE, TILE), BF16)
    vj[CT] = jnp.zeros((PW, TILE), BF16)
    row(z, own[...])

    s = slot((2, 0))
    from_plane(s)
    plane(colbuf.at[s], s, (0, 1), 10)
    plane(colbuf.at[s], s, (0, 3), 11)
    s = slot((0, 2))
    from_plane(s)
    plane(colbuf.at[s], s, (1, 0), 12)
    plane(colbuf.at[s], s, (3, 0), 13)
    s = slot((2 * (1 - core), 2 * core))
    plane(colbuf.at[s], s, (2 * core, 2 * (1 - core)), 14)
    s = (z + 6) % NZ
    from_line(s)
    line(rowbuf.at[s], s, 1, 4)
    line(rowbuf.at[s], s, 2, 5)
    s = (z + 2) % NZ
    from_line(s)
    line(rowbuf.at[s], s, 7, 6)
    for d in two:
        forward(colbuf.at[slot(d)], slot(d))

    for o in range(1, NZ):
        zz = (z + o) % NZ
        remote(flags.at[0], flagbuf.at[zz], gsend.at[o], grecv.at[zz], sibling).wait_recv()
    flagbuf[z] = flags[z]
    for zz in range(NZ):
        mask[3 * zz : 3 * zz + 3, :] = flagbuf[zz].astype(F32)[0:3, :]
    lists_of(mask[...], z, lists, info)
    column(me, own[...])
    for d in two:
        column(slot(d), colbuf[slot(d)])
    for d in near:
        from_plane(slot(d))
        forward(colbuf.at[slot(d)], slot(d))
        column(slot(d), colbuf[slot(d)])
    for o in (2, 6, 1, 7):
        zz = (z + o) % NZ
        if o in (1, 7):
            from_line(zz)
        row(zz, rowbuf[zz])
    first = ((0, 0),) + two + near
    for d in first[:3]:
        s = slot(d, 1 - core)
        from_sibling(s)
        column(s, colbuf[s])
    for d in far:
        from_plane(slot(d))
        forward(colbuf.at[slot(d)], slot(d))
    for d in far:
        column(slot(d), colbuf[slot(d)])
    for d in first[3:]:
        s = slot(d, 1 - core)
        from_sibling(s)
        column(s, colbuf[s])
    for o in (3, 5, 4):
        zz = (z + o) % NZ
        from_line(zz)
        row(zz, rowbuf[zz])
    for d in far:
        s = slot(d, 1 - core)
        from_sibling(s)
        column(s, colbuf[s])
    for copy in sent:
        copy.wait_send()


JT = 8
SUB = 8


def apply_kernel(lists, info, xj, vj, xi, out, *held):
    out[...] = jnp.zeros_like(out)

    def weights(p):
        return jnp.concatenate([xi[info[p, 0]], xi[info[p, 1]]], axis=1)

    def compute(p, k, q, w, held_ref):
        s = jnp.dot(xj[lists[p, k + q]], w, preferred_element_type=F32)
        held_ref[q * TILE : (q + 1) * TILE, :] = jnp.exp(jnp.minimum(s, 0.0)).astype(BF16)

    def apply(p, k, q, held_ref):
        v = jnp.concatenate([vj[lists[p, k + q]], vj[lists[p, k + q + 1]]], axis=1)
        return jnp.dot(v, held_ref[q * TILE : (q + 2) * TILE, :], preferred_element_type=F32)

    def following(p, k):
        end = k + JT >= info[p, 2]
        last = p == PAIRS - 1
        k = jnp.where(end, jnp.where(last, 100, 0), k + JT)
        return jnp.where(end & ~last, p + 1, p), k

    total = sum(jnp.maximum((info[p, 2] + JT - 1) // JT, 1) for p in range(PAIRS))
    zero = jnp.int32(0)
    w = weights(zero)
    for q in range(JT):
        compute(zero, zero, q, w, held[SUB - 1])

    def step(_, at):
        for u in range(SUB):
            nxt = following(*at)
            w = weights(nxt[0])
            r = None
            for q in range(JT):
                compute(*nxt, q, w, held[u])
                if q % 2 == 0:
                    part = apply(*at, q, held[u - 1])
                    r = part if r is None else r + part
            a, b = info[at[0], 0], info[at[0], 1]
            out[a] += r[:, :TILE]
            out[b] += r[:, TILE:]
            at = nxt
        return at

    lax.fori_loop(0, (total + SUB - 1) // SUB, step, (zero, zero))


def reduce_kernel(part, xj, vj, xi, out, got, held, total, send, recv):
    x, y, z, core = place()
    barrier = pltpu.get_barrier_semaphore()
    for o in range(1, NZ):
        pl.semaphore_signal(barrier, inc=1, device_id=device(x, y, (z + o) % NZ, core), device_id_type=MESH)
    pl.semaphore_wait(barrier, NZ - 1)

    def copy(o, slot):
        to = (z + o) % NZ
        return pltpu.make_async_remote_copy(
            src_ref=part.at[pl.ds(3 * to, 3)],
            dst_ref=got.at[slot],
            send_sem=send.at[o],
            recv_sem=recv.at[slot],
            device_id=device(x, y, to, core),
            device_id_type=MESH,
        )

    for o in (4, 3, 5, 2, 6, 1, 7):
        copy(o, z).start()

    w = jnp.concatenate([xi[3 * z + q] for q in range(3)], axis=1)
    some = 8

    def compute(j, q, slot):
        s = jnp.dot(xj[j * some + q], w, preferred_element_type=F32)
        held[slot, q * TILE : (q + 1) * TILE, :] = jnp.exp(jnp.minimum(s, 0.0)).astype(BF16)

    def apply(j, q, slot):
        v = jnp.concatenate([vj[j * some + q], vj[j * some + q + 1]], axis=1)
        return jnp.dot(v, held[slot, q * TILE : (q + 2) * TILE, :], preferred_element_type=F32)

    for q in range(some):
        compute(0, q, 1)

    def step(t, acc):
        for u in range(4):
            j = 4 * t + u
            for q in range(some):
                compute(jnp.minimum(j + 1, CT // some - 1), q, u % 2)
                if q % 2 == 0:
                    acc = acc + apply(j, q, 1 - u % 2)
        return acc

    total[...] = lax.fori_loop(0, CT // some // 4, step, jnp.zeros((PW, BLK), F32))
    for o in (1, 7, 2, 6, 3, 5, 4):
        zz = (z + o) % NZ
        copy(o, zz).wait_recv()
        for q in range(3):
            total[:, q * TILE : (q + 1) * TILE] += got[zz, q]
    out[...] = total[...]
    for o in range(1, NZ):
        copy(o, z).wait_send()


def local(points, panel, tile_pairs):
    shape = jax.ShapeDtypeStruct
    dma = pltpu.SemaphoreType.DMA
    xj, vj, xi, lists, info = pl.pallas_call(
        gather_kernel,
        out_shape=(
            shape((CT + 1, TILE, TILE), BF16),
            shape((CT + 1, PW, TILE), BF16),
            shape((RT, TILE, TILE), BF16),
            shape((16, 128), jnp.int32),
            shape((16, 128), jnp.int32),
        ),
        in_specs=[HBM] * 3,
        out_specs=[VMEM] * 5,
        scratch_shapes=[
            pltpu.VMEM((D + PW, BLK), BF16),
            pltpu.VMEM((RT, CT * NZ), jnp.int32),
            pltpu.VMEM((PLANE, D + PW, BLK), BF16),
            pltpu.VMEM((NZ, D + PW, BLK), BF16),
            pltpu.VMEM((NZ, 16, 128), BF16),
            pltpu.VMEM((NZ, 16, 128), BF16),
            pltpu.VMEM((RT, 128), F32),
            dma((3,)),
            dma((16,)),
            dma((PLANE,)),
            dma((PLANE,)),
            dma((PLANE,)),
            dma((NZ,)),
            dma((NZ,)),
            dma((NZ,)),
            dma((NZ,)),
        ],
        compiler_params=pltpu.CompilerParams(
            collective_id=0, has_side_effects=True, vmem_limit_bytes=40 * 2**20
        ),
        name="gather",
    )(*(pltpu.with_memory_space_constraint(a, pltpu.HBM) for a in (points.T, panel.T, tile_pairs)))
    part = pl.pallas_call(
        apply_kernel,
        out_shape=shape((RT, PW, TILE), F32),
        in_specs=[SMEM, SMEM, VMEM, VMEM, VMEM],
        out_specs=VMEM,
        scratch_shapes=[pltpu.VMEM((JT * TILE, 2 * TILE), BF16)] * SUB,
        compiler_params=pltpu.CompilerParams(vmem_limit_bytes=40 * 2**20),
        name="apply",
    )(lists, info, xj, vj, xi)
    return pl.pallas_call(
        reduce_kernel,
        out_shape=shape((PW, BLK), F32),
        in_specs=[VMEM] * 4,
        out_specs=VMEM,
        scratch_shapes=[
            pltpu.VMEM((NZ, 3, PW, TILE), F32),
            pltpu.VMEM((2, 8 * TILE, BLK), BF16),
            pltpu.VMEM((PW, BLK), F32),
            dma((NZ,)),
            dma((NZ,)),
        ],
        compiler_params=pltpu.CompilerParams(
            collective_id=1, has_side_effects=True, vmem_limit_bytes=40 * 2**20
        ),
        name="reduce",
    )(part, xj, vj, xi).T


def solution(mesh):
    in_specs = (P(("row", "col"), None), P(("row", "col"), None), P("row", None))
    out_specs = P(("row", "col"), None)
    return jax.shard_map(local, mesh=mesh, in_specs=in_specs, out_specs=out_specs, check_vma=False)
```

```python
import jax
import jax.numpy as jnp
from jax import lax
from jax.experimental import pallas as pl
from jax.experimental.pallas import tpu as pltpu
from jax.sharding import PartitionSpec as P

D = 64
PW = 16
TILE = 128
BLK = 384
NX, NY, NZ = 4, 4, 8
PLANE = NX * NY * 2
CT = 3 * PLANE
RT = 3 * NZ
PAIRS = (RT - 2) // 2
BIG = 9984.0
F32, BF16 = jnp.float32, jnp.bfloat16
MESH = pl.DeviceIdType.MESH
VMEM = pl.BlockSpec(memory_space=pltpu.VMEM)
HBM = pl.BlockSpec(memory_space=pltpu.HBM)
SMEM = pl.BlockSpec(memory_space=pltpu.SMEM)


def place():
    row, col = lax.axis_index("row"), lax.axis_index("col")
    x = (col // 4) * 2 + row // 16
    return x, col % 4, (row // 2) % 8, row % 2


def device(x, y, z, core):
    return ((x % 2) * 16 + z * 2 + core, (x // 2) * 4 + y)


def slot_of(x, y, core):
    return (x % 2) * 16 + core * 8 + (x // 2) * 4 + y


def iota(shape, dim):
    return lax.broadcasted_iota(jnp.int32, shape, dim)


def norm_parts(x_t):
    floats = x_t.astype(F32)
    n = jnp.sum(floats * floats, axis=0, keepdims=True) * (-1.0 / 32.0)
    hi = n.astype(BF16).astype(F32)
    rest = n - hi
    mid = rest.astype(BF16).astype(F32)
    return hi, mid, rest - mid


def mix(rows, first, hi, mid, lo, other):
    one = jnp.where((rows >= other) & (rows < other + 3), 1.0, 0.0)
    return jnp.where(rows == first, hi, jnp.where(rows == first + 1, mid, jnp.where(rows == first + 2, lo, one)))


def lists_of(m, z, list_ref, info_ref):
    gram = lax.dot_general(m, m, (((1,), (1,)), ((), ())), preferred_element_type=F32)
    sub, lane = iota((RT, RT), 0), iota((RT, RT), 1)
    eye = sub == lane
    n_col = jnp.sum(m, axis=1, keepdims=True)
    n_row = jnp.sum(jnp.where(eye, gram, 0.0), axis=0, keepdims=True)
    apart = n_col + n_row - 2.0 * gram

    def key_of(overlap, apart0, ids, axis):
        score = jnp.where(apart0 > 0.5, overlap * 32.0 - ids.astype(F32), -1e6)
        return score == jnp.max(score, axis=axis, keepdims=True)

    o_row, a_row = gram[0:1, :], apart[0:1, :]
    o_col, a_col = gram[:, 0:1], apart[:, 0:1]
    e_row = key_of(o_row, a_row, lane[0:1, :], 1)
    e_col = key_of(o_col, a_col, sub[:, 0:1], 0)
    p_col = jnp.sum(jnp.where(e_row, gram, 0.0), axis=1, keepdims=True)
    p_row = jnp.sum(jnp.where(e_col, gram, 0.0), axis=0, keepdims=True)

    def order(o, p, a):
        return jnp.where(a < 0.5, 0.0, jnp.where(p > o, 1e4 - o, 2e4 + o))

    def mine(ids):
        return (ids >= 3 * z) & (ids < 3 * z + 3)

    k_row = jnp.where(mine(lane[0:1, :]), 1e6, order(o_row, p_row, a_row))
    k_col = jnp.where(mine(sub[:, 0:1]), 1e6, order(o_col, p_col, a_col))
    before = (k_col < k_row) | ((k_col == k_row) & (sub < lane))
    rank = jnp.sum(before.astype(F32), axis=0, keepdims=True)
    pair = iota((16, RT), 0).astype(F32)
    even = jnp.where(rank == 2.0 * pair, 1.0, 0.0)
    odd = jnp.where(rank == 2.0 * pair + 1.0, 1.0, 0.0)
    m = jnp.where(mine(iota((RT, 128), 0)), 0.0, m)
    both = jnp.maximum(
        jnp.dot(even, m, preferred_element_type=F32), jnp.dot(odd, m, preferred_element_type=F32)
    )
    tri = jnp.where(iota((128, 128), 0) < iota((128, 128), 1), 1.0, 0.0)
    pos = jnp.dot(both, tri, preferred_element_type=F32)
    count = jnp.sum(both, axis=1, keepdims=True)
    where = jnp.where(both > 0.5, pos, -1.0)
    ids = iota((16, 128), 1)
    k = iota((128, 128), 0).astype(F32)
    prow = iota((16, 128), 0)
    total = jnp.where(ids.astype(F32) >= count, float(CT), 0.0)
    for p in range(PAIRS):
        hit = jnp.where(where[p : p + 1, :] == k, 1.0, 0.0)
        got = lax.dot_general(ids.astype(F32), hit, (((1,), (1,)), ((), ())), preferred_element_type=F32)
        total = total + jnp.where(prow == p, got, 0.0)
    list_ref[...] = total.astype(jnp.int32)
    t = iota((16, RT), 1).astype(F32)
    first = jnp.sum(even * t, axis=1, keepdims=True)
    second = jnp.sum(odd * t, axis=1, keepdims=True)
    info = jnp.where(ids == 0, first, jnp.where(ids == 1, second, jnp.where(ids == 2, count, 0.0)))
    info_ref[...] = info.astype(jnp.int32)


def gather_kernel(
    pts, pan, tp, xj, vj, xi, lists, info,
    own, pairs, colbuf, rowbuf, flags, flagbuf, up, down, mask, local, psend, precv, fsend, frecv, zsend, zrecv, gsend, grecv,
):
    x, y, z, core = place()
    c = (x // 2) * 4 + y
    me = slot_of(x, y, core)

    def at(d):
        return (x + d[0]) % 4, (y + d[1]) % 4

    def slot(d, which=core):
        return slot_of(*at(d), which)

    fetch = [
        pltpu.make_async_copy(pts, own.at[0:D], local.at[0]),
        pltpu.make_async_copy(pan, own.at[D : D + PW], local.at[1]),
        pltpu.make_async_copy(tp, pairs, local.at[2]),
    ]
    for copy in fetch:
        copy.start()
    barrier = pltpu.get_barrier_semaphore()
    near = ((1, 0), (3, 0), (0, 1), (0, 3), (1, 1), (1, 3), (3, 1), (3, 3))
    two = ((2, 0), (0, 2))
    far = ((2, 1), (2, 3), (1, 2), (3, 2), (2, 2))
    for d in two + near:
        pl.semaphore_signal(barrier, inc=1, device_id=device(*at(d), z, core), device_id_type=MESH)
    for o in (1, 2, 6, 7):
        pl.semaphore_signal(barrier, inc=1, device_id=device(x, y, (z + o) % NZ, core), device_id_type=MESH)
    pl.semaphore_signal(barrier, inc=1, device_id=device(x, y, z, 1 - core), device_id_type=MESH)

    for copy in fetch:
        copy.wait()
    r, t = iota((16, 24), 0), iota((16, 24), 1)
    pick = jnp.where((r < 3) & (t == 3 * c + r), 1.0, 0.0)
    rows = jnp.dot(pick, pairs[...].astype(F32), preferred_element_type=F32)
    for zz in range(NZ):
        low = rows[:, 48 * zz : 48 * zz + 48]
        high = rows[:, BLK + 48 * zz : BLK + 48 * zz + 48]
        flags[(zz - z + NZ) % NZ] = jnp.concatenate([low, high, jnp.zeros((16, 32), F32)], axis=1).astype(BF16)
    pl.semaphore_wait(barrier, 10 + 4 + 1)

    def remote(src, dst, send, recv, to):
        return pltpu.make_async_remote_copy(
            src_ref=src, dst_ref=dst, send_sem=send, recv_sem=recv, device_id=to, device_id_type=MESH
        )

    sent = []

    def start(copy):
        copy.start()
        sent.append(copy)

    def plane(src, s, d, i):
        start(remote(src, colbuf.at[s], psend.at[i], precv.at[s], device(*at(d), z, core)))

    def line(src, s, o, i):
        start(remote(src, rowbuf.at[s], zsend.at[i], zrecv.at[s], device(x, y, (z + o) % NZ, core)))

    sibling = device(x, y, z, 1 - core)

    def forward(src, s):
        start(remote(src, colbuf.at[s], fsend.at[s], frecv.at[s], sibling))

    def from_plane(s):
        remote(own, colbuf.at[s], psend.at[0], precv.at[s], sibling).wait_recv()

    def from_line(s):
        remote(own.at[0:D], rowbuf.at[s], zsend.at[0], zrecv.at[s], sibling).wait_recv()

    def from_sibling(s):
        remote(own, colbuf.at[s], fsend.at[s], frecv.at[s], sibling).wait_recv()

    def flag(src, dst, o, i, s):
        start(remote(src, dst, gsend.at[i], grecv.at[s], device(x, y, (z + o) % NZ, core)))

    def from_flag(dst, s):
        remote(dst, dst, gsend.at[0], grecv.at[s], sibling).wait_recv()

    flag(flags.at[2:5], up, 2, 0, NZ)
    flag(flags.at[5:7], down, 6, 1, NZ + 1)
    flag(flags.at[1], flagbuf.at[z], 1, 2, z)
    flag(flags.at[7], flagbuf.at[z], 7, 3, z)
    for i, o in enumerate((2, 6, 1, 7)):
        line(own.at[0:D], z, o, i)
    for i, d in enumerate(two + near):
        plane(own, me, d, i)
    forward(own, me)

    row64 = iota((64, TILE), 0)

    def row(zz, block):
        hi, mid, lo = norm_parts(block[0:D, :])
        for q in range(3):
            cut = slice(q * TILE, (q + 1) * TILE)
            tail = mix(row64, 0, hi[:, cut], mid[:, cut], lo[:, cut], 3)
            tail = jnp.where(row64 == 8 + 3 * zz + q, 1.0, tail)
            xi[3 * zz + q, 0:D, :] = block[0:D, cut] * jnp.bfloat16(1.0 / 16.0)
            xi[3 * zz + q, D:128, :] = tail.astype(BF16)

    lanes = iota((RT, 128), 1)

    def column(s, block):
        hi, mid, lo = norm_parts(block[0:D, :])
        for q in range(3):
            cut = slice(q * TILE, (q + 1) * TILE)
            tail = mix(row64[0:8], 3, hi[:, cut], mid[:, cut], lo[:, cut], 0)
            on = jnp.sum(jnp.where(lanes == 3 * s + q, mask[...], 0.0), axis=1, keepdims=True)
            off = jnp.broadcast_to((on - 1.0) * BIG, (RT, TILE))
            feats = jnp.concatenate(
                [block[0:D, cut].astype(F32), tail, off, jnp.zeros((128 - D - 8 - RT, TILE), F32)], axis=0
            )
            xj[3 * s + q] = feats.T.astype(BF16)
            vj[3 * s + q] = block[D:, cut]

    xj[CT] = jnp.zeros((TILE, TILE), BF16)
    vj[CT] = jnp.zeros((PW, TILE), BF16)
    row(z, own[...])
    below, above = (z + 6) % NZ, (z + 2) % NZ
    from_flag(up, NZ)
    flag(up.at[1], flagbuf.at[below], 1, 4, below)
    flag(up.at[2], flagbuf.at[below], 2, 5, below)
    from_flag(down, NZ + 1)
    flag(down.at[0], flagbuf.at[above], 7, 6, above)

    s = slot((2, 0))
    from_plane(s)
    plane(colbuf.at[s], s, (0, 1), 10)
    plane(colbuf.at[s], s, (0, 3), 11)
    s = slot((0, 2))
    from_plane(s)
    plane(colbuf.at[s], s, (1, 0), 12)
    plane(colbuf.at[s], s, (3, 0), 13)
    s = slot((2 * (1 - core), 2 * core))
    plane(colbuf.at[s], s, (2 * core, 2 * (1 - core)), 14)
    from_line(below)
    line(rowbuf.at[below], below, 1, 4)
    line(rowbuf.at[below], below, 2, 5)
    from_line(above)
    line(rowbuf.at[above], above, 7, 6)
    for d in two:
        forward(colbuf.at[slot(d)], slot(d))
    side, diagonal = near[:4], near[4:]
    for d in side:
        from_plane(slot(d))
        forward(colbuf.at[slot(d)], slot(d))
    row(below, rowbuf[below])
    row(above, rowbuf[above])
    for o in (1, 7):
        zz = (z + o) % NZ
        from_line(zz)
        row(zz, rowbuf[zz])

    for d in diagonal:
        from_plane(slot(d))
        forward(colbuf.at[slot(d)], slot(d))

    for o in (1, 7, 3, 4, 5):
        from_flag(flagbuf.at[(z + o) % NZ], (z + o) % NZ)
    flagbuf[z] = flags[0]
    flagbuf[below] = up[0]
    flagbuf[above] = down[1]
    for zz in range(NZ):
        mask[3 * zz : 3 * zz + 3, :] = flagbuf[zz].astype(F32)[0:3, :]
    column(me, own[...])
    for d in two + side + diagonal:
        column(slot(d), colbuf[slot(d)])

    def other(d):
        s = slot(d, 1 - core)
        from_sibling(s)
        column(s, colbuf[s])

    lists_of(mask[...], z, lists, info)
    for d in far:
        from_plane(slot(d))
        forward(colbuf.at[slot(d)], slot(d))
    for d in ((0, 0),) + two + side:
        other(d)
    for d in diagonal:
        other(d)
    for o in (3, 5, 4):
        zz = (z + o) % NZ
        from_line(zz)
        row(zz, rowbuf[zz])
    for d in far:
        column(slot(d), colbuf[slot(d)])
    for d in far:
        other(d)
    for copy in sent:
        copy.wait_send()


JT = 8
STEPS = (16, 4)
HELD = 4


def apply_kernel(lists, info, xj, vj, xi, out, *held):
    out[...] = jnp.zeros_like(out)

    def weights(p):
        return jnp.concatenate([xi[info[p, 0]], xi[info[p, 1]]], axis=1)

    def compute(p, k, q, w, held_ref):
        s = jnp.dot(xj[lists[p, k + q]], w, preferred_element_type=F32)
        held_ref[q * TILE : (q + 1) * TILE, :] = jnp.exp(jnp.minimum(s, 0.0)).astype(BF16)

    def apply(p, k, q, held_ref):
        v = jnp.concatenate([vj[lists[p, k + q]], vj[lists[p, k + q + 1]]], axis=1)
        return jnp.dot(v, held_ref[q * TILE : (q + 2) * TILE, :], preferred_element_type=F32)

    def following(p, k):
        end = k + JT >= info[p, 2]
        last = p == PAIRS - 1
        k = jnp.where(end, jnp.where(last, 100, 0), k + JT)
        return jnp.where(end & ~last, p + 1, p), k

    total = sum(jnp.maximum((info[p, 2] + JT - 1) // JT, 1) for p in range(PAIRS))
    zero = jnp.int32(0)
    w = weights(zero)
    for q in range(JT):
        compute(zero, zero, q, w, held[HELD - 1])

    def steps(some):
        def step(_, at):
            for u in range(some):
                nxt = following(*at)
                w = weights(nxt[0])
                r = None
                for q in range(JT):
                    compute(*nxt, q, w, held[u % HELD])
                    if q % 2 == 0:
                        part = apply(*at, q, held[(u - 1) % HELD])
                        r = part if r is None else r + part
                a, b = info[at[0], 0], info[at[0], 1]
                out[a] += r[:, :TILE]
                out[b] += r[:, TILE:]
                at = nxt
            return at

        return step

    many, few = STEPS
    whole = total // many
    at = lax.fori_loop(0, whole, steps(many), (zero, zero))
    lax.fori_loop(0, (total - whole * many + few - 1) // few, steps(few), at)


def reduce_kernel(part, xj, vj, xi, out, got, held, total, send, recv):
    x, y, z, core = place()
    barrier = pltpu.get_barrier_semaphore()
    for o in range(1, NZ):
        pl.semaphore_signal(barrier, inc=1, device_id=device(x, y, (z + o) % NZ, core), device_id_type=MESH)
    pl.semaphore_wait(barrier, NZ - 1)

    def copy(o, slot):
        to = (z + o) % NZ
        return pltpu.make_async_remote_copy(
            src_ref=part.at[pl.ds(3 * to, 3)],
            dst_ref=got.at[slot],
            send_sem=send.at[o],
            recv_sem=recv.at[slot],
            device_id=device(x, y, to, core),
            device_id_type=MESH,
        )

    for o in (4, 3, 5, 2, 6, 1, 7):
        copy(o, z).start()

    w = jnp.concatenate([xi[3 * z + q] for q in range(3)], axis=1)
    some = 8

    def compute(j, q, slot):
        s = jnp.dot(xj[j * some + q], w, preferred_element_type=F32)
        held[slot, q * TILE : (q + 1) * TILE, :] = jnp.exp(jnp.minimum(s, 0.0)).astype(BF16)

    def apply(j, q, slot):
        v = jnp.concatenate([vj[j * some + q], vj[j * some + q + 1]], axis=1)
        return jnp.dot(v, held[slot, q * TILE : (q + 2) * TILE, :], preferred_element_type=F32)

    for q in range(some):
        compute(0, q, 1)

    def step(t, acc):
        for u in range(4):
            j = 4 * t + u
            for q in range(some):
                compute(jnp.minimum(j + 1, CT // some - 1), q, u % 2)
                if q % 2 == 0:
                    acc = acc + apply(j, q, 1 - u % 2)
        return acc

    total[...] = lax.fori_loop(0, CT // some // 4, step, jnp.zeros((PW, BLK), F32))
    for o in (1, 7, 2, 6, 3, 5, 4):
        zz = (z + o) % NZ
        copy(o, zz).wait_recv()
        for q in range(3):
            total[:, q * TILE : (q + 1) * TILE] += got[zz, q]
    out[...] = total[...]
    for o in range(1, NZ):
        copy(o, z).wait_send()


def local(points, panel, tile_pairs):
    shape = jax.ShapeDtypeStruct
    dma = pltpu.SemaphoreType.DMA
    xj, vj, xi, lists, info = pl.pallas_call(
        gather_kernel,
        out_shape=(
            shape((CT + 1, TILE, TILE), BF16),
            shape((CT + 1, PW, TILE), BF16),
            shape((RT, TILE, TILE), BF16),
            shape((16, 128), jnp.int32),
            shape((16, 128), jnp.int32),
        ),
        in_specs=[HBM] * 3,
        out_specs=[VMEM] * 5,
        scratch_shapes=[
            pltpu.VMEM((D + PW, BLK), BF16),
            pltpu.VMEM((RT, CT * NZ), jnp.int32),
            pltpu.VMEM((PLANE, D + PW, BLK), BF16),
            pltpu.VMEM((NZ, D, BLK), BF16),
            pltpu.VMEM((NZ, 16, 128), BF16),
            pltpu.VMEM((NZ, 16, 128), BF16),
            pltpu.VMEM((3, 16, 128), BF16),
            pltpu.VMEM((2, 16, 128), BF16),
            pltpu.VMEM((RT, 128), F32),
            dma((3,)),
            dma((16,)),
            dma((PLANE,)),
            dma((PLANE,)),
            dma((PLANE,)),
            dma((NZ,)),
            dma((NZ,)),
            dma((NZ,)),
            dma((NZ + 2,)),
        ],
        compiler_params=pltpu.CompilerParams(
            collective_id=0, has_side_effects=True, vmem_limit_bytes=40 * 2**20
        ),
        name="gather",
    )(*(pltpu.with_memory_space_constraint(a, pltpu.HBM) for a in (points.T, panel.T, tile_pairs)))
    part = pl.pallas_call(
        apply_kernel,
        out_shape=shape((RT, PW, TILE), F32),
        in_specs=[SMEM, SMEM, VMEM, VMEM, VMEM],
        out_specs=VMEM,
        scratch_shapes=[pltpu.VMEM((JT * TILE, 2 * TILE), BF16)] * HELD,
        compiler_params=pltpu.CompilerParams(vmem_limit_bytes=40 * 2**20),
        name="apply",
    )(lists, info, xj, vj, xi)
    return pl.pallas_call(
        reduce_kernel,
        out_shape=shape((PW, BLK), F32),
        in_specs=[VMEM] * 4,
        out_specs=VMEM,
        scratch_shapes=[
            pltpu.VMEM((NZ, 3, PW, TILE), F32),
            pltpu.VMEM((2, 8 * TILE, BLK), BF16),
            pltpu.VMEM((PW, BLK), F32),
            dma((NZ,)),
            dma((NZ,)),
        ],
        compiler_params=pltpu.CompilerParams(
            collective_id=1, has_side_effects=True, vmem_limit_bytes=40 * 2**20
        ),
        name="reduce",
    )(part, xj, vj, xi).T


def solution(mesh):
    in_specs = (P(("row", "col"), None), P(("row", "col"), None), P("row", None))
    out_specs = P(("row", "col"), None)
    return jax.shard_map(local, mesh=mesh, in_specs=in_specs, out_specs=out_specs, check_vma=False)
```

```python
import jax
import jax.numpy as jnp
from jax import lax
from jax.experimental import pallas as pl
from jax.experimental.pallas import tpu as pltpu
from jax.sharding import PartitionSpec as P

D = 64
PW = 16
TILE = 128
BLK = 384
NX, NY, NZ = 4, 4, 8
PLANE = NX * NY * 2
CT = 3 * PLANE
RT = 3 * NZ
PAIRS = (RT - 2) // 2
BIG = 9984.0
F32, BF16 = jnp.float32, jnp.bfloat16
MESH = pl.DeviceIdType.MESH
VMEM = pl.BlockSpec(memory_space=pltpu.VMEM)
HBM = pl.BlockSpec(memory_space=pltpu.HBM)
SMEM = pl.BlockSpec(memory_space=pltpu.SMEM)


def place():
    row, col = lax.axis_index("row"), lax.axis_index("col")
    x = (col // 4) * 2 + row // 16
    return x, col % 4, (row // 2) % 8, row % 2


def device(x, y, z, core):
    return ((x % 2) * 16 + z * 2 + core, (x // 2) * 4 + y)


def slot_of(x, y, core):
    return (x % 2) * 16 + core * 8 + (x // 2) * 4 + y


def iota(shape, dim):
    return lax.broadcasted_iota(jnp.int32, shape, dim)


def norm_parts(x_t):
    floats = x_t.astype(F32)
    n = jnp.sum(floats * floats, axis=0, keepdims=True) * (-1.0 / 32.0)
    hi = n.astype(BF16).astype(F32)
    rest = n - hi
    mid = rest.astype(BF16).astype(F32)
    return hi, mid, rest - mid


def mix(rows, first, hi, mid, lo, other):
    one = jnp.where((rows >= other) & (rows < other + 3), 1.0, 0.0)
    return jnp.where(rows == first, hi, jnp.where(rows == first + 1, mid, jnp.where(rows == first + 2, lo, one)))


def lists_of(m, z, list_ref, info_ref):
    gram = lax.dot_general(m, m, (((1,), (1,)), ((), ())), preferred_element_type=F32)
    sub, lane = iota((RT, RT), 0), iota((RT, RT), 1)
    eye = sub == lane
    n_col = jnp.sum(m, axis=1, keepdims=True)
    n_row = jnp.sum(jnp.where(eye, gram, 0.0), axis=0, keepdims=True)
    apart = n_col + n_row - 2.0 * gram

    def key_of(overlap, apart0, ids, axis):
        score = jnp.where(apart0 > 0.5, overlap * 32.0 - ids.astype(F32), -1e6)
        return score == jnp.max(score, axis=axis, keepdims=True)

    o_row, a_row = gram[0:1, :], apart[0:1, :]
    o_col, a_col = gram[:, 0:1], apart[:, 0:1]
    e_row = key_of(o_row, a_row, lane[0:1, :], 1)
    e_col = key_of(o_col, a_col, sub[:, 0:1], 0)
    p_col = jnp.sum(jnp.where(e_row, gram, 0.0), axis=1, keepdims=True)
    p_row = jnp.sum(jnp.where(e_col, gram, 0.0), axis=0, keepdims=True)

    def order(o, p, a):
        return jnp.where(a < 0.5, 0.0, jnp.where(p > o, 1e4 - o, 2e4 + o))

    def mine(ids):
        return (ids >= 3 * z) & (ids < 3 * z + 3)

    k_row = jnp.where(mine(lane[0:1, :]), 1e6, order(o_row, p_row, a_row))
    k_col = jnp.where(mine(sub[:, 0:1]), 1e6, order(o_col, p_col, a_col))
    before = (k_col < k_row) | ((k_col == k_row) & (sub < lane))
    rank = jnp.sum(before.astype(F32), axis=0, keepdims=True)
    pair = iota((16, RT), 0).astype(F32)
    even = jnp.where(rank == 2.0 * pair, 1.0, 0.0)
    odd = jnp.where(rank == 2.0 * pair + 1.0, 1.0, 0.0)
    m = jnp.where(mine(iota((RT, 128), 0)), 0.0, m)
    both = jnp.maximum(
        jnp.dot(even, m, preferred_element_type=F32), jnp.dot(odd, m, preferred_element_type=F32)
    )
    tri = jnp.where(iota((128, 128), 0) < iota((128, 128), 1), 1.0, 0.0)
    pos = jnp.dot(both, tri, preferred_element_type=F32)
    count = jnp.sum(both, axis=1, keepdims=True)
    where = jnp.where(both > 0.5, pos, -1.0)
    ids = iota((16, 128), 1)
    k = iota((128, 128), 0).astype(F32)
    prow = iota((16, 128), 0)
    total = jnp.where(ids.astype(F32) >= count, float(CT), 0.0)
    for p in range(PAIRS):
        hit = jnp.where(where[p : p + 1, :] == k, 1.0, 0.0)
        got = lax.dot_general(ids.astype(F32), hit, (((1,), (1,)), ((), ())), preferred_element_type=F32)
        total = total + jnp.where(prow == p, got, 0.0)
    list_ref[...] = total.astype(jnp.int32)
    t = iota((16, RT), 1).astype(F32)
    first = jnp.sum(even * t, axis=1, keepdims=True)
    second = jnp.sum(odd * t, axis=1, keepdims=True)
    info = jnp.where(ids == 0, first, jnp.where(ids == 1, second, jnp.where(ids == 2, count, 0.0)))
    info_ref[...] = info.astype(jnp.int32)


def gather_kernel(
    pts, pan, tp, xj, vj, xi, lists, info,
    own, pairs, colbuf, rowbuf, flags, flagbuf, up, down, mask, away, local, psend, precv, fsend, frecv, zsend, zrecv, gsend, grecv,
):
    x, y, z, core = place()
    c = (x // 2) * 4 + y
    me = slot_of(x, y, core)

    def at(d):
        return (x + d[0]) % 4, (y + d[1]) % 4

    def slot(d, which=core):
        return slot_of(*at(d), which)

    fetch = [
        pltpu.make_async_copy(pts, own.at[0:D], local.at[0]),
        pltpu.make_async_copy(pan, own.at[D : D + PW], local.at[1]),
        pltpu.make_async_copy(tp, pairs, local.at[2]),
    ]
    for copy in fetch:
        copy.start()
    barrier = pltpu.get_barrier_semaphore()
    near = ((1, 0), (3, 0), (0, 1), (0, 3), (1, 1), (1, 3), (3, 1), (3, 3))
    two = ((2, 0), (0, 2))
    far = ((2, 1), (2, 3), (1, 2), (3, 2), (2, 2))
    for d in two + near:
        pl.semaphore_signal(barrier, inc=1, device_id=device(*at(d), z, core), device_id_type=MESH)
    for o in (1, 2, 6, 7):
        pl.semaphore_signal(barrier, inc=1, device_id=device(x, y, (z + o) % NZ, core), device_id_type=MESH)
    pl.semaphore_signal(barrier, inc=1, device_id=device(x, y, z, 1 - core), device_id_type=MESH)

    for copy in fetch:
        copy.wait()
    r, t = iota((16, 24), 0), iota((16, 24), 1)
    pick = jnp.where((r < 3) & (t == 3 * c + r), 1.0, 0.0).astype(BF16)
    rows = jnp.dot(pick, pairs[...].astype(BF16), preferred_element_type=F32)
    for zz in range(NZ):
        low = rows[:, 48 * zz : 48 * zz + 48]
        high = rows[:, BLK + 48 * zz : BLK + 48 * zz + 48]
        flags[(zz - z + NZ) % NZ] = jnp.concatenate([low, high, jnp.zeros((16, 32), F32)], axis=1).astype(BF16)
    pl.semaphore_wait(barrier, 10 + 4 + 1)

    def remote(src, dst, send, recv, to):
        return pltpu.make_async_remote_copy(
            src_ref=src, dst_ref=dst, send_sem=send, recv_sem=recv, device_id=to, device_id_type=MESH
        )

    sent = []

    def start(copy):
        copy.start()
        sent.append(copy)

    def plane(src, s, d, i):
        start(remote(src, colbuf.at[s], psend.at[i], precv.at[s], device(*at(d), z, core)))

    def line(src, s, o, i):
        start(remote(src, rowbuf.at[s], zsend.at[i], zrecv.at[s], device(x, y, (z + o) % NZ, core)))

    sibling = device(x, y, z, 1 - core)

    def forward(src, s):
        start(remote(src, colbuf.at[s], fsend.at[s], frecv.at[s], sibling))

    def from_plane(s):
        remote(own, colbuf.at[s], psend.at[0], precv.at[s], sibling).wait_recv()

    def from_line(s):
        remote(own.at[0:D], rowbuf.at[s], zsend.at[0], zrecv.at[s], sibling).wait_recv()

    def from_sibling(s):
        remote(own, colbuf.at[s], fsend.at[s], frecv.at[s], sibling).wait_recv()

    def flag(src, dst, o, i, s):
        start(remote(src, dst, gsend.at[i], grecv.at[s], device(x, y, (z + o) % NZ, core)))

    def from_flag(dst, s):
        remote(dst, dst, gsend.at[0], grecv.at[s], sibling).wait_recv()

    flag(flags.at[2:5], up, 2, 0, NZ)
    flag(flags.at[5:7], down, 6, 1, NZ + 1)
    flag(flags.at[1], flagbuf.at[z], 1, 2, z)
    flag(flags.at[7], flagbuf.at[z], 7, 3, z)
    for i, o in enumerate((2, 6, 1, 7)):
        line(own.at[0:D], z, o, i)
    for i, d in enumerate(two + near):
        plane(own, me, d, i)
    forward(own, me)

    row64 = iota((64, TILE), 0)

    def row(zz, block):
        hi, mid, lo = norm_parts(block[0:D, :])
        for q in range(3):
            cut = slice(q * TILE, (q + 1) * TILE)
            tail = mix(row64, 0, hi[:, cut], mid[:, cut], lo[:, cut], 3)
            tail = jnp.where(row64 == 8 + 3 * zz + q, 1.0, tail)
            xi[3 * zz + q, 0:D, :] = block[0:D, cut] * jnp.bfloat16(1.0 / 16.0)
            xi[3 * zz + q, D:128, :] = tail.astype(BF16)

    lanes = iota((RT, 128), 1)

    def column(s, block):
        hi, mid, lo = norm_parts(block[0:D, :])
        for q in range(3):
            cut = slice(q * TILE, (q + 1) * TILE)
            tail = mix(row64[0:8], 3, hi[:, cut], mid[:, cut], lo[:, cut], 0)
            off = jnp.sum(jnp.where(lanes == 3 * s + q, away[...], 0.0), axis=1, keepdims=True)
            off = jnp.broadcast_to(off, (RT, TILE))
            tail = jnp.concatenate([tail, off, jnp.zeros((128 - D - 8 - RT, TILE), F32)], axis=0)
            xj[3 * s + q] = jnp.concatenate([block[0:D, cut], tail.astype(BF16)], axis=0).T
            vj[3 * s + q] = block[D:, cut]

    xj[CT] = jnp.zeros((TILE, TILE), BF16)
    vj[CT] = jnp.zeros((PW, TILE), BF16)
    row(z, own[...])
    below, above = (z + 6) % NZ, (z + 2) % NZ
    from_flag(up, NZ)
    flag(up.at[1], flagbuf.at[below], 1, 4, below)
    flag(up.at[2], flagbuf.at[below], 2, 5, below)
    from_flag(down, NZ + 1)
    flag(down.at[0], flagbuf.at[above], 7, 6, above)

    s = slot((2, 0))
    from_plane(s)
    plane(colbuf.at[s], s, (0, 1), 10)
    plane(colbuf.at[s], s, (0, 3), 11)
    s = slot((0, 2))
    from_plane(s)
    plane(colbuf.at[s], s, (1, 0), 12)
    plane(colbuf.at[s], s, (3, 0), 13)
    s = slot((2 * (1 - core), 2 * core))
    plane(colbuf.at[s], s, (2 * core, 2 * (1 - core)), 14)
    from_line(below)
    line(rowbuf.at[below], below, 1, 4)
    line(rowbuf.at[below], below, 2, 5)
    from_line(above)
    line(rowbuf.at[above], above, 7, 6)
    for d in two:
        forward(colbuf.at[slot(d)], slot(d))
    side, diagonal = near[:4], near[4:]
    for d in side:
        from_plane(slot(d))
        forward(colbuf.at[slot(d)], slot(d))
    row(below, rowbuf[below])
    row(above, rowbuf[above])
    for o in (1, 7):
        zz = (z + o) % NZ
        from_line(zz)
        row(zz, rowbuf[zz])

    for d in diagonal:
        from_plane(slot(d))
        forward(colbuf.at[slot(d)], slot(d))

    for o in (1, 7, 3, 4, 5):
        from_flag(flagbuf.at[(z + o) % NZ], (z + o) % NZ)
    flagbuf[z] = flags[0]
    flagbuf[below] = up[0]
    flagbuf[above] = down[1]
    for zz in range(NZ):
        mask[3 * zz : 3 * zz + 3, :] = flagbuf[zz].astype(F32)[0:3, :]
    away[...] = (mask[...] - 1.0) * BIG
    column(me, own[...])
    for d in two + side + diagonal:
        column(slot(d), colbuf[slot(d)])

    def other(d):
        s = slot(d, 1 - core)
        from_sibling(s)
        column(s, colbuf[s])

    lists_of(mask[...], z, lists, info)
    for d in far:
        from_plane(slot(d))
        forward(colbuf.at[slot(d)], slot(d))
    for d in ((0, 0),) + two + side:
        other(d)
    for d in diagonal:
        other(d)
    for o in (3, 5, 4):
        zz = (z + o) % NZ
        from_line(zz)
        row(zz, rowbuf[zz])
    for d in far:
        column(slot(d), colbuf[slot(d)])
    for d in far:
        other(d)
    for copy in sent:
        copy.wait_send()


JT = 8
STEPS = (16, 4)
HELD = 4


def apply_kernel(lists, info, xj, vj, xi, out, *held):
    out[...] = jnp.zeros_like(out)

    def weights(p):
        return jnp.concatenate([xi[info[p, 0]], xi[info[p, 1]]], axis=1)

    def compute(p, k, q, w, held_ref):
        s = jnp.dot(xj[lists[p, k + q]], w, preferred_element_type=F32)
        held_ref[q * TILE : (q + 1) * TILE, :] = jnp.exp(jnp.minimum(s, 0.0)).astype(BF16)

    def apply(p, k, q, held_ref):
        v = jnp.concatenate([vj[lists[p, k + q]], vj[lists[p, k + q + 1]]], axis=1)
        return jnp.dot(v, held_ref[q * TILE : (q + 2) * TILE, :], preferred_element_type=F32)

    def following(p, k):
        end = k + JT >= info[p, 2]
        last = p == PAIRS - 1
        k = jnp.where(end, jnp.where(last, 100, 0), k + JT)
        return jnp.where(end & ~last, p + 1, p), k

    total = sum(jnp.maximum((info[p, 2] + JT - 1) // JT, 1) for p in range(PAIRS))
    zero = jnp.int32(0)
    w = weights(zero)
    for q in range(JT):
        compute(zero, zero, q, w, held[HELD - 1])

    def steps(some):
        def step(_, at):
            for u in range(some):
                nxt = following(*at)
                w = weights(nxt[0])
                r = None
                for q in range(JT):
                    compute(*nxt, q, w, held[u % HELD])
                    if q % 2 == 0:
                        part = apply(*at, q, held[(u - 1) % HELD])
                        r = part if r is None else r + part
                a, b = info[at[0], 0], info[at[0], 1]
                out[a] += r[:, :TILE]
                out[b] += r[:, TILE:]
                at = nxt
            return at

        return step

    many, few = STEPS
    whole = total // many
    at = lax.fori_loop(0, whole, steps(many), (zero, zero))
    lax.fori_loop(0, (total - whole * many + few - 1) // few, steps(few), at)


def reduce_kernel(part, xj, vj, xi, out, got, held, total, send, recv):
    x, y, z, core = place()
    barrier = pltpu.get_barrier_semaphore()
    for o in (4, 3, 5, 2, 6, 1, 7):
        pl.semaphore_signal(barrier, inc=1, device_id=device(x, y, (z + o) % NZ, core), device_id_type=MESH)
    pl.semaphore_wait(barrier, NZ - 1)

    def copy(o, slot):
        to = (z + o) % NZ
        return pltpu.make_async_remote_copy(
            src_ref=part.at[pl.ds(3 * to, 3)],
            dst_ref=got.at[slot],
            send_sem=send.at[o],
            recv_sem=recv.at[slot],
            device_id=device(x, y, to, core),
            device_id_type=MESH,
        )

    for o in (4, 3, 5, 2, 6, 1, 7):
        copy(o, z).start()

    w = jnp.concatenate([xi[3 * z + q] for q in range(3)], axis=1)
    some = 8

    def compute(j, q, slot):
        s = jnp.dot(xj[j * some + q], w, preferred_element_type=F32)
        held[slot, q * TILE : (q + 1) * TILE, :] = jnp.exp(jnp.minimum(s, 0.0)).astype(BF16)

    def apply(j, q, slot):
        v = jnp.concatenate([vj[j * some + q], vj[j * some + q + 1]], axis=1)
        return jnp.dot(v, held[slot, q * TILE : (q + 2) * TILE, :], preferred_element_type=F32)

    for q in range(some):
        compute(0, q, 1)

    def step(t, acc):
        for u in range(4):
            j = 4 * t + u
            for q in range(some):
                compute(jnp.minimum(j + 1, CT // some - 1), q, u % 2)
                if q % 2 == 0:
                    acc = acc + apply(j, q, 1 - u % 2)
        return acc

    total[...] = lax.fori_loop(0, CT // some // 4, step, jnp.zeros((PW, BLK), F32))
    for o in (1, 7, 2, 6, 3, 5, 4):
        zz = (z + o) % NZ
        copy(o, zz).wait_recv()
        for q in range(3):
            total[:, q * TILE : (q + 1) * TILE] += got[zz, q]
    out[...] = total[...]
    for o in range(1, NZ):
        copy(o, z).wait_send()


def local(points, panel, tile_pairs):
    shape = jax.ShapeDtypeStruct
    dma = pltpu.SemaphoreType.DMA
    xj, vj, xi, lists, info = pl.pallas_call(
        gather_kernel,
        out_shape=(
            shape((CT + 1, TILE, TILE), BF16),
            shape((CT + 1, PW, TILE), BF16),
            shape((RT, TILE, TILE), BF16),
            shape((16, 128), jnp.int32),
            shape((16, 128), jnp.int32),
        ),
        in_specs=[HBM] * 3,
        out_specs=[VMEM] * 5,
        scratch_shapes=[
            pltpu.VMEM((D + PW, BLK), BF16),
            pltpu.VMEM((RT, CT * NZ), jnp.int32),
            pltpu.VMEM((PLANE, D + PW, BLK), BF16),
            pltpu.VMEM((NZ, D, BLK), BF16),
            pltpu.VMEM((NZ, 16, 128), BF16),
            pltpu.VMEM((NZ, 16, 128), BF16),
            pltpu.VMEM((3, 16, 128), BF16),
            pltpu.VMEM((2, 16, 128), BF16),
            pltpu.VMEM((RT, 128), F32),
            pltpu.VMEM((RT, 128), F32),
            dma((3,)),
            dma((16,)),
            dma((PLANE,)),
            dma((PLANE,)),
            dma((PLANE,)),
            dma((NZ,)),
            dma((NZ,)),
            dma((NZ,)),
            dma((NZ + 2,)),
        ],
        compiler_params=pltpu.CompilerParams(
            collective_id=0, has_side_effects=True, vmem_limit_bytes=40 * 2**20
        ),
        name="gather",
    )(*(pltpu.with_memory_space_constraint(a, pltpu.HBM) for a in (points.T, panel.T, tile_pairs)))
    part = pl.pallas_call(
        apply_kernel,
        out_shape=shape((RT, PW, TILE), F32),
        in_specs=[SMEM, SMEM, VMEM, VMEM, VMEM],
        out_specs=VMEM,
        scratch_shapes=[pltpu.VMEM((JT * TILE, 2 * TILE), BF16)] * HELD,
        compiler_params=pltpu.CompilerParams(vmem_limit_bytes=40 * 2**20),
        name="apply",
    )(lists, info, xj, vj, xi)
    return pl.pallas_call(
        reduce_kernel,
        out_shape=shape((PW, BLK), F32),
        in_specs=[VMEM] * 4,
        out_specs=VMEM,
        scratch_shapes=[
            pltpu.VMEM((NZ, 3, PW, TILE), F32),
            pltpu.VMEM((2, 8 * TILE, BLK), BF16),
            pltpu.VMEM((PW, BLK), F32),
            dma((NZ,)),
            dma((NZ,)),
        ],
        compiler_params=pltpu.CompilerParams(
            collective_id=1, has_side_effects=True, vmem_limit_bytes=40 * 2**20
        ),
        name="reduce",
    )(part, xj, vj, xi).T


def solution(mesh):
    in_specs = (P(("row", "col"), None), P(("row", "col"), None), P("row", None))
    out_specs = P(("row", "col"), None)
    return jax.shard_map(local, mesh=mesh, in_specs=in_specs, out_specs=out_specs, check_vma=False)
```

```python
import jax
import jax.numpy as jnp
from jax import lax
from jax.experimental import pallas as pl
from jax.experimental.pallas import tpu as pltpu
from jax.sharding import PartitionSpec as P

D = 64
PW = 16
TILE = 128
BLK = 384
NX, NY, NZ = 4, 4, 8
PLANE = NX * NY * 2
CT = 3 * PLANE
RT = 3 * NZ
PAIRS = (RT - 2) // 2
BIG = 9984.0
F32, BF16 = jnp.float32, jnp.bfloat16
MESH = pl.DeviceIdType.MESH
VMEM = pl.BlockSpec(memory_space=pltpu.VMEM)
HBM = pl.BlockSpec(memory_space=pltpu.HBM)
SMEM = pl.BlockSpec(memory_space=pltpu.SMEM)


def place():
    row, col = lax.axis_index("row"), lax.axis_index("col")
    x = (col // 4) * 2 + row // 16
    return x, col % 4, (row // 2) % 8, row % 2


def device(x, y, z, core):
    return ((x % 2) * 16 + z * 2 + core, (x // 2) * 4 + y)


def slot_of(x, y, core):
    return (x % 2) * 16 + core * 8 + (x // 2) * 4 + y


def iota(shape, dim):
    return lax.broadcasted_iota(jnp.int32, shape, dim)


def norm_parts(x_t):
    floats = x_t.astype(F32)
    n = jnp.sum(floats * floats, axis=0, keepdims=True) * (-1.0 / 32.0)
    hi = n.astype(BF16).astype(F32)
    rest = n - hi
    mid = rest.astype(BF16).astype(F32)
    return hi, mid, rest - mid


def mix(rows, first, hi, mid, lo, other):
    one = jnp.where((rows >= other) & (rows < other + 3), 1.0, 0.0)
    return jnp.where(rows == first, hi, jnp.where(rows == first + 1, mid, jnp.where(rows == first + 2, lo, one)))


def lists_of(m, z, list_ref, info_ref):
    gram = lax.dot_general(m, m, (((1,), (1,)), ((), ())), preferred_element_type=F32)
    sub, lane = iota((RT, RT), 0), iota((RT, RT), 1)
    eye = sub == lane
    n_col = jnp.sum(m, axis=1, keepdims=True)
    n_row = jnp.sum(jnp.where(eye, gram, 0.0), axis=0, keepdims=True)
    apart = n_col + n_row - 2.0 * gram

    def key_of(overlap, apart0, ids, axis):
        score = jnp.where(apart0 > 0.5, overlap * 32.0 - ids.astype(F32), -1e6)
        return score == jnp.max(score, axis=axis, keepdims=True)

    o_row, a_row = gram[0:1, :], apart[0:1, :]
    o_col, a_col = gram[:, 0:1], apart[:, 0:1]
    e_row = key_of(o_row, a_row, lane[0:1, :], 1)
    e_col = key_of(o_col, a_col, sub[:, 0:1], 0)
    p_col = jnp.sum(jnp.where(e_row, gram, 0.0), axis=1, keepdims=True)
    p_row = jnp.sum(jnp.where(e_col, gram, 0.0), axis=0, keepdims=True)

    def order(o, p, a):
        return jnp.where(a < 0.5, 0.0, jnp.where(p > o, 1e4 - o, 2e4 + o))

    def mine(ids):
        return (ids >= 3 * z) & (ids < 3 * z + 3)

    k_row = jnp.where(mine(lane[0:1, :]), 1e6, order(o_row, p_row, a_row))
    k_col = jnp.where(mine(sub[:, 0:1]), 1e6, order(o_col, p_col, a_col))
    before = (k_col < k_row) | ((k_col == k_row) & (sub < lane))
    rank = jnp.sum(before.astype(F32), axis=0, keepdims=True)
    pair = iota((16, RT), 0).astype(F32)
    even = jnp.where(rank == 2.0 * pair, 1.0, 0.0)
    odd = jnp.where(rank == 2.0 * pair + 1.0, 1.0, 0.0)
    m = jnp.where(mine(iota((RT, 128), 0)), 0.0, m)
    both = jnp.maximum(
        jnp.dot(even, m, preferred_element_type=F32), jnp.dot(odd, m, preferred_element_type=F32)
    )
    tri = jnp.where(iota((128, 128), 0) < iota((128, 128), 1), 1.0, 0.0)
    pos = jnp.dot(both, tri, preferred_element_type=F32)
    count = jnp.sum(both, axis=1, keepdims=True)
    where = jnp.where(both > 0.5, pos, -1.0)
    ids = iota((16, 128), 1)
    k = iota((128, 128), 0).astype(F32)
    prow = iota((16, 128), 0)
    total = jnp.where(ids.astype(F32) >= count, float(CT), 0.0)
    for p in range(PAIRS):
        hit = jnp.where(where[p : p + 1, :] == k, 1.0, 0.0)
        got = lax.dot_general(ids.astype(F32), hit, (((1,), (1,)), ((), ())), preferred_element_type=F32)
        total = total + jnp.where(prow == p, got, 0.0)
    list_ref[...] = total.astype(jnp.int32)
    t = iota((16, RT), 1).astype(F32)
    first = jnp.sum(even * t, axis=1, keepdims=True)
    second = jnp.sum(odd * t, axis=1, keepdims=True)
    info = jnp.where(ids == 0, first, jnp.where(ids == 1, second, jnp.where(ids == 2, count, 0.0)))
    info_ref[...] = info.astype(jnp.int32)


def gather_kernel(
    pts, pan, tp, xj, vj, xi, lists, info,
    own, pairs, colbuf, rowbuf, flags, flagbuf, up, down, mask, away, local, psend, precv, fsend, frecv, zsend, zrecv, gsend, grecv,
):
    x, y, z, core = place()
    c = (x // 2) * 4 + y
    me = slot_of(x, y, core)

    def at(d):
        return (x + d[0]) % 4, (y + d[1]) % 4

    def slot(d, which=core):
        return slot_of(*at(d), which)

    fetch = [
        pltpu.make_async_copy(pts, own.at[0:D], local.at[0]),
        pltpu.make_async_copy(pan, own.at[D : D + PW], local.at[1]),
        pltpu.make_async_copy(tp, pairs, local.at[2]),
    ]
    for copy in fetch:
        copy.start()
    barrier = pltpu.get_barrier_semaphore()
    near = ((1, 0), (3, 0), (0, 1), (0, 3), (1, 1), (1, 3), (3, 1), (3, 3))
    two = ((2, 0), (0, 2))
    far = ((2, 1), (2, 3), (1, 2), (3, 2), (2, 2))
    for d in two + near:
        pl.semaphore_signal(barrier, inc=1, device_id=device(*at(d), z, core), device_id_type=MESH)
    for o in (1, 2, 6, 7):
        pl.semaphore_signal(barrier, inc=1, device_id=device(x, y, (z + o) % NZ, core), device_id_type=MESH)
    pl.semaphore_signal(barrier, inc=1, device_id=device(x, y, z, 1 - core), device_id_type=MESH)

    for copy in fetch:
        copy.wait()
    r, t = iota((16, 24), 0), iota((16, 24), 1)
    pick = jnp.where((r < 3) & (t == 3 * c + r), 1.0, 0.0).astype(BF16)
    rows = jnp.dot(pick, pairs[...].astype(BF16), preferred_element_type=F32)
    for zz in range(NZ):
        low = rows[:, 48 * zz : 48 * zz + 48]
        high = rows[:, BLK + 48 * zz : BLK + 48 * zz + 48]
        flags[(zz - z + NZ) % NZ] = jnp.concatenate([low, high, jnp.zeros((16, 32), F32)], axis=1).astype(BF16)
    pl.semaphore_wait(barrier, 10 + 4 + 1)

    def remote(src, dst, send, recv, to):
        return pltpu.make_async_remote_copy(
            src_ref=src, dst_ref=dst, send_sem=send, recv_sem=recv, device_id=to, device_id_type=MESH
        )

    sent = []

    def start(copy):
        copy.start()
        sent.append(copy)

    def plane(src, s, d, i):
        start(remote(src, colbuf.at[s], psend.at[i], precv.at[s], device(*at(d), z, core)))

    def line(src, s, o, i):
        start(remote(src, rowbuf.at[s], zsend.at[i], zrecv.at[s], device(x, y, (z + o) % NZ, core)))

    sibling = device(x, y, z, 1 - core)

    def forward(src, s):
        start(remote(src, colbuf.at[s], fsend.at[s], frecv.at[s], sibling))

    def from_plane(s):
        remote(own, colbuf.at[s], psend.at[0], precv.at[s], sibling).wait_recv()

    def from_line(s):
        remote(own.at[0:D], rowbuf.at[s], zsend.at[0], zrecv.at[s], sibling).wait_recv()

    def from_sibling(s):
        remote(own, colbuf.at[s], fsend.at[s], frecv.at[s], sibling).wait_recv()

    def flag(src, dst, o, i, s):
        start(remote(src, dst, gsend.at[i], grecv.at[s], device(x, y, (z + o) % NZ, core)))

    def from_flag(dst, s):
        remote(dst, dst, gsend.at[0], grecv.at[s], sibling).wait_recv()

    flag(flags.at[2:5], up, 2, 0, NZ)
    flag(flags.at[5:7], down, 6, 1, NZ + 1)
    flag(flags.at[1], flagbuf.at[z], 1, 2, z)
    flag(flags.at[7], flagbuf.at[z], 7, 3, z)
    for i, o in enumerate((2, 6, 1, 7)):
        line(own.at[0:D], z, o, i)
    for i, d in enumerate(two + near):
        plane(own, me, d, i)
    forward(own, me)

    row64 = iota((64, TILE), 0)

    def row(zz, block):
        hi, mid, lo = norm_parts(block[0:D, :])
        for q in range(3):
            cut = slice(q * TILE, (q + 1) * TILE)
            tail = mix(row64, 0, hi[:, cut], mid[:, cut], lo[:, cut], 3)
            tail = jnp.where(row64 == 8 + 3 * zz + q, 1.0, tail)
            xi[3 * zz + q, 0:D, :] = block[0:D, cut] * jnp.bfloat16(1.0 / 16.0)
            xi[3 * zz + q, D:128, :] = tail.astype(BF16)

    lanes = iota((RT, 128), 1)

    def column(s, block):
        hi, mid, lo = norm_parts(block[0:D, :])
        for q in range(3):
            cut = slice(q * TILE, (q + 1) * TILE)
            tail = mix(row64[0:8], 3, hi[:, cut], mid[:, cut], lo[:, cut], 0)
            off = jnp.sum(jnp.where(lanes == 3 * s + q, away[...], 0.0), axis=1, keepdims=True)
            off = jnp.broadcast_to(off, (RT, TILE))
            tail = jnp.concatenate([tail, off, jnp.zeros((128 - D - 8 - RT, TILE), F32)], axis=0)
            xj[3 * s + q] = jnp.concatenate([block[0:D, cut], tail.astype(BF16)], axis=0).T
            vj[3 * s + q] = block[D:, cut]

    xj[CT] = jnp.zeros((TILE, TILE), BF16)
    vj[CT] = jnp.zeros((PW, TILE), BF16)
    row(z, own[...])
    below, above = (z + 6) % NZ, (z + 2) % NZ
    from_flag(up, NZ)
    flag(up.at[1], flagbuf.at[below], 1, 4, below)
    flag(up.at[2], flagbuf.at[below], 2, 5, below)
    from_flag(down, NZ + 1)
    flag(down.at[0], flagbuf.at[above], 7, 6, above)

    s = slot((2, 0))
    from_plane(s)
    plane(colbuf.at[s], s, (0, 1), 10)
    plane(colbuf.at[s], s, (0, 3), 11)
    s = slot((0, 2))
    from_plane(s)
    plane(colbuf.at[s], s, (1, 0), 12)
    plane(colbuf.at[s], s, (3, 0), 13)
    s = slot((2 * (1 - core), 2 * core))
    plane(colbuf.at[s], s, (2 * core, 2 * (1 - core)), 14)
    from_line(below)
    line(rowbuf.at[below], below, 1, 4)
    line(rowbuf.at[below], below, 2, 5)
    from_line(above)
    line(rowbuf.at[above], above, 7, 6)
    for d in two:
        forward(colbuf.at[slot(d)], slot(d))
    side, diagonal = near[:4], near[4:]
    for d in side:
        from_plane(slot(d))
        forward(colbuf.at[slot(d)], slot(d))
    row(below, rowbuf[below])
    row(above, rowbuf[above])
    for o in (1, 7):
        zz = (z + o) % NZ
        from_line(zz)
        row(zz, rowbuf[zz])

    for d in diagonal:
        from_plane(slot(d))
        forward(colbuf.at[slot(d)], slot(d))

    for o in (1, 7, 3, 4, 5):
        from_flag(flagbuf.at[(z + o) % NZ], (z + o) % NZ)
    flagbuf[z] = flags[0]
    flagbuf[below] = up[0]
    flagbuf[above] = down[1]
    for zz in range(NZ):
        mask[3 * zz : 3 * zz + 3, :] = flagbuf[zz].astype(F32)[0:3, :]
    away[...] = (mask[...] - 1.0) * BIG
    column(me, own[...])
    for d in two + side + diagonal:
        column(slot(d), colbuf[slot(d)])

    def other(d):
        s = slot(d, 1 - core)
        from_sibling(s)
        column(s, colbuf[s])

    lists_of(mask[...], z, lists, info)
    for d in far:
        from_plane(slot(d))
        forward(colbuf.at[slot(d)], slot(d))
    for d in ((0, 0),) + two + side:
        other(d)
    for d in diagonal:
        other(d)
    for o in (3, 5, 4):
        zz = (z + o) % NZ
        from_line(zz)
        row(zz, rowbuf[zz])
    for d in far:
        column(slot(d), colbuf[slot(d)])
    for d in far:
        other(d)
    for copy in sent:
        copy.wait_send()


JT = 8
STEPS = (16, 2)
HELD = 2


def apply_kernel(lists, info, xj, vj, xi, out, *held):
    out[...] = jnp.zeros_like(out)

    def weights(p):
        return jnp.concatenate([xi[info[p, 0]], xi[info[p, 1]]], axis=1)

    def compute(p, k, q, w, held_ref):
        s = jnp.dot(xj[lists[p, k + q]], w, preferred_element_type=F32)
        held_ref[q * TILE : (q + 1) * TILE, :] = jnp.exp(jnp.minimum(s, 0.0)).astype(BF16)

    def apply(p, k, q, held_ref):
        v = jnp.concatenate([vj[lists[p, k + q]], vj[lists[p, k + q + 1]]], axis=1)
        return jnp.dot(v, held_ref[q * TILE : (q + 2) * TILE, :], preferred_element_type=F32)

    def following(p, k):
        end = k + JT >= info[p, 2]
        last = p == PAIRS - 1
        k = jnp.where(end, jnp.where(last, 100, 0), k + JT)
        return jnp.where(end & ~last, p + 1, p), k

    total = sum(jnp.maximum((info[p, 2] + JT - 1) // JT, 1) for p in range(PAIRS))
    zero = jnp.int32(0)
    w = weights(zero)
    for q in range(JT):
        compute(zero, zero, q, w, held[HELD - 1])

    def steps(some):
        def step(_, at):
            for u in range(some):
                nxt = following(*at)
                w = weights(nxt[0])
                r = None
                for q in range(JT):
                    compute(*nxt, q, w, held[u % HELD])
                    if q % 2 == 0:
                        part = apply(*at, q, held[(u - 1) % HELD])
                        r = part if r is None else r + part
                a, b = info[at[0], 0], info[at[0], 1]
                out[a] += r[:, :TILE]
                out[b] += r[:, TILE:]
                at = nxt
            return at

        return step

    many, few = STEPS
    whole = total // many
    at = lax.fori_loop(0, whole, steps(many), (zero, zero))
    lax.fori_loop(0, (total - whole * many + few - 1) // few, steps(few), at)


def reduce_kernel(part, xj, vj, xi, out, got, held, total, send, recv):
    x, y, z, core = place()
    barrier = pltpu.get_barrier_semaphore()
    for o in (4, 3, 5, 2, 6, 1, 7):
        pl.semaphore_signal(barrier, inc=1, device_id=device(x, y, (z + o) % NZ, core), device_id_type=MESH)
    pl.semaphore_wait(barrier, NZ - 1)

    def copy(o, slot):
        to = (z + o) % NZ
        return pltpu.make_async_remote_copy(
            src_ref=part.at[pl.ds(3 * to, 3)],
            dst_ref=got.at[slot],
            send_sem=send.at[o],
            recv_sem=recv.at[slot],
            device_id=device(x, y, to, core),
            device_id_type=MESH,
        )

    for o in (4, 3, 5, 2, 6, 1, 7):
        copy(o, z).start()

    w = jnp.concatenate([xi[3 * z + q] for q in range(3)], axis=1)
    some = 8

    def compute(j, q, slot):
        s = jnp.dot(xj[j * some + q], w, preferred_element_type=F32)
        held[slot, q * TILE : (q + 1) * TILE, :] = jnp.exp(jnp.minimum(s, 0.0)).astype(BF16)

    def apply(j, q, slot):
        v = jnp.concatenate([vj[j * some + q], vj[j * some + q + 1]], axis=1)
        return jnp.dot(v, held[slot, q * TILE : (q + 2) * TILE, :], preferred_element_type=F32)

    for q in range(some):
        compute(0, q, 1)

    def step(t, acc):
        for u in range(4):
            j = 4 * t + u
            for q in range(some):
                compute(jnp.minimum(j + 1, CT // some - 1), q, u % 2)
                if q % 2 == 0:
                    acc = acc + apply(j, q, 1 - u % 2)
        return acc

    total[...] = lax.fori_loop(0, CT // some // 4, step, jnp.zeros((PW, BLK), F32))
    for o in (1, 7, 2, 6, 3, 5, 4):
        zz = (z + o) % NZ
        copy(o, zz).wait_recv()
        for q in range(3):
            total[:, q * TILE : (q + 1) * TILE] += got[zz, q]
    out[...] = total[...]
    for o in range(1, NZ):
        copy(o, z).wait_send()


def local(points, panel, tile_pairs):
    shape = jax.ShapeDtypeStruct
    dma = pltpu.SemaphoreType.DMA
    xj, vj, xi, lists, info = pl.pallas_call(
        gather_kernel,
        out_shape=(
            shape((CT + 1, TILE, TILE), BF16),
            shape((CT + 1, PW, TILE), BF16),
            shape((RT, TILE, TILE), BF16),
            shape((16, 128), jnp.int32),
            shape((16, 128), jnp.int32),
        ),
        in_specs=[HBM] * 3,
        out_specs=[VMEM] * 5,
        scratch_shapes=[
            pltpu.VMEM((D + PW, BLK), BF16),
            pltpu.VMEM((RT, CT * NZ), jnp.int32),
            pltpu.VMEM((PLANE, D + PW, BLK), BF16),
            pltpu.VMEM((NZ, D, BLK), BF16),
            pltpu.VMEM((NZ, 16, 128), BF16),
            pltpu.VMEM((NZ, 16, 128), BF16),
            pltpu.VMEM((3, 16, 128), BF16),
            pltpu.VMEM((2, 16, 128), BF16),
            pltpu.VMEM((RT, 128), F32),
            pltpu.VMEM((RT, 128), F32),
            dma((3,)),
            dma((16,)),
            dma((PLANE,)),
            dma((PLANE,)),
            dma((PLANE,)),
            dma((NZ,)),
            dma((NZ,)),
            dma((NZ,)),
            dma((NZ + 2,)),
        ],
        compiler_params=pltpu.CompilerParams(
            collective_id=0, has_side_effects=True, vmem_limit_bytes=40 * 2**20
        ),
        name="gather",
    )(*(pltpu.with_memory_space_constraint(a, pltpu.HBM) for a in (points.T, panel.T, tile_pairs)))
    part = pl.pallas_call(
        apply_kernel,
        out_shape=shape((RT, PW, TILE), F32),
        in_specs=[SMEM, SMEM, VMEM, VMEM, VMEM],
        out_specs=VMEM,
        scratch_shapes=[pltpu.VMEM((JT * TILE, 2 * TILE), BF16)] * HELD,
        compiler_params=pltpu.CompilerParams(vmem_limit_bytes=40 * 2**20),
        name="apply",
    )(lists, info, xj, vj, xi)
    return pl.pallas_call(
        reduce_kernel,
        out_shape=shape((PW, BLK), F32),
        in_specs=[VMEM] * 4,
        out_specs=VMEM,
        scratch_shapes=[
            pltpu.VMEM((NZ, 3, PW, TILE), F32),
            pltpu.VMEM((2, 8 * TILE, BLK), BF16),
            pltpu.VMEM((PW, BLK), F32),
            dma((NZ,)),
            dma((NZ,)),
        ],
        compiler_params=pltpu.CompilerParams(
            collective_id=1, has_side_effects=True, vmem_limit_bytes=40 * 2**20
        ),
        name="reduce",
    )(part, xj, vj, xi).T


def solution(mesh):
    in_specs = (P(("row", "col"), None), P(("row", "col"), None), P("row", None))
    out_specs = P(("row", "col"), None)
    return jax.shard_map(local, mesh=mesh, in_specs=in_specs, out_specs=out_specs, check_vma=False)
```
